256 devices in a mesh: dp: 16 (over x, y), tensor: 16 (over z, core).
Axes of the slice: x: 4, y: 4, z: 8, core: 2. Of those that a mesh axis runs over, the one named last changes fastest.
Arguments:
- activations: bfloat16 [12288, 8192], P('dp', 'tensor'), may hold values from -6 to 6
- query_gradient: bfloat16 [12288, 8192], P('dp', 'tensor'), may hold values from -6 to 6
- query_matrix: bfloat16 [8192, 8192], P(None, 'tensor'), may hold values from -0.09375 to 0.09375
- down_table_rows: bfloat16 [64, 16, 8192], P('dp', None, 'tensor'), may hold values from -3 to 3
- up_table_rows: bfloat16 [64, 16, 8192], P('dp', None, 'tensor'), may hold values from -3 to 3
- adapter_per_group: int32 [96], P('dp'), may hold values from 0 to 63
- slot_of_adapter: int32 [64], replicated, may hold values from 0 to 63, each once
Outputs:
- token_gradient: float32 [12288, 8192], P('dp', 'tensor')
- down_after_step: bfloat16 [64, 16, 8192], P(None, None, 'tensor')
- up_after_step: bfloat16 [64, 16, 8192], P(None, None, 'tensor')
The draws below stay inside these ranges and needn't reach their ends.
Inputs may be any that keep to these rules, and one draw needn't show every extreme that they name: `slot_of_adapter`: each id appears once.
All inputs are finite; a program needn't handle non-finite values.
Results may differ from the reference program's by a relative error of at most 0.0015.
Values may be sent and summed in bfloat16 or wider, within the bound.
A program may use at most 128 MiB of HBM per device.

```python
import math
import jax
import jax.numpy as jnp
import numpy as np
from jax import lax

MODEL_WIDTH = 8192
QUERY_WIDTH = 8192
ADAPTER_RANK = 16
ADAPTER_COUNT = 64
GROUP = 128
TOKEN_COUNT = 12288
GROUPS = 96


def set_ends(result, key, least, top_value):
    shape = result.shape
    spot = [jax.random.randint(jax.random.fold_in(key, axis), (), 0, shape[axis]) for axis in range(len(shape))]
    result = result.at[tuple(spot)].set(least)
    longest = shape.index(max(shape))
    spot[longest] = (spot[longest] + 1) % shape[longest]
    return result.at[tuple(spot)].set(top_value)


def raised(drawn, stream_key, source, target, shards_of, factor):
    owner, partner = [(jnp.arange(drawn.shape[position]) // (drawn.shape[position] // shards_of)).reshape([-1 if axis == position else 1 for axis in range(drawn.ndim)]) for position in (source, target)]
    chosen = jax.random.permutation(stream_key, shards_of)[partner]
    strong = (owner == chosen) | (owner == (partner + shards_of // 2) % shards_of)
    return jnp.where(strong, factor * drawn, drawn)


def block_scale(key, dims, pieces, least, top_value):
    level, own = 1.0, jax.random.fold_in(key, 6)
    for dim, blocks in pieces:
        heights = jnp.exp(jax.random.uniform(jax.random.fold_in(own, dim), (blocks,), jnp.float32, least / len(pieces), top_value / len(pieces)))
        level = level * jnp.repeat(heights, dims[dim] // blocks).reshape([-1 if axis == dim else 1 for axis in range(len(dims))])
    return level


def cumulative_ranks(number_of, skew):
    weights = [(1 << 20) // math.isqrt(standing ** skew) + 1 for standing in range(1, number_of + 1)]
    spread = 1 + sum(weights) // (1 << 30)
    return np.cumsum(np.array([max(1, weight // spread) for weight in weights]))


def ranked_ids(stream_key, dims, amount, slope):
    table = cumulative_ranks(amount, slope)
    ticket = jax.random.randint(jax.random.fold_in(stream_key, 1), dims, 0, int(table[amount - 1]))
    grade = jnp.searchsorted(jnp.asarray(table, jnp.int32), ticket, side="right")
    return jax.random.permutation(jax.random.fold_in(stream_key, 2), amount)[grade].astype(jnp.int32)


def centred(own_key, extent, scale, reach, split=(), held_as=jnp.bfloat16):
    drawn = jax.random.normal(own_key, extent, jnp.float32) * scale
    if len(split) > 0:
        drawn = block_scale(own_key, extent, split, -0.22, 0.18) * drawn
    return jnp.clip(drawn, min=-reach, max=reach).astype(held_as)


def gaussian_with(own_key, dims, deviation, most, shards, heavy, kind=jnp.bfloat16):
    entries = deviation * jax.random.normal(own_key, dims, jnp.float32)
    if shards:
        entries = entries * block_scale(own_key, dims, shards, -0.22, 0.18)
    return jnp.clip(raised(entries, jax.random.fold_in(own_key, 3), *heavy), -most, most).astype(kind)


def setup_inputs(seed: int = 0) -> dict:
    splits = jax.random.split(jax.random.key(seed), 8)
    activations = centred(splits[0], (TOKEN_COUNT, MODEL_WIDTH), 1.0, 6.0, ((0, 16), (1, 16)))
    query_gradient = centred(splits[1], (TOKEN_COUNT, QUERY_WIDTH), 1.0, 6.0, ((0, 16), (1, 16)))
    query_matrix = gaussian_with(splits[2], (MODEL_WIDTH, QUERY_WIDTH), QUERY_WIDTH ** -0.5, 0.09375, ((1, 16),), (1, 0, 16, 2.0))
    down_table_rows = centred(splits[3], (ADAPTER_COUNT, ADAPTER_RANK, MODEL_WIDTH), 0.5, 3.0, ((0, 16), (2, 16)))
    up_table_rows = centred(splits[4], (ADAPTER_COUNT, ADAPTER_RANK, QUERY_WIDTH), 0.5, 3.0, ((0, 16), (2, 16)))
    adapter_per_group = set_ends(ranked_ids(splits[5], (GROUPS,), ADAPTER_COUNT, 2), jax.random.fold_in(splits[5], 3), 0, ADAPTER_COUNT - 1).astype(jnp.int32)
    slot_of_adapter = jax.random.permutation(splits[6], ADAPTER_COUNT).astype(jnp.int32)
    return dict(activations=activations, query_gradient=query_gradient, query_matrix=query_matrix, down_table_rows=down_table_rows, up_table_rows=up_table_rows, adapter_per_group=adapter_per_group, slot_of_adapter=slot_of_adapter)


adapter_scale = 0.25
learning_rate = 1.5

def reference(activations, query_gradient, query_matrix, down_table_rows, up_table_rows, adapter_per_group, slot_of_adapter):
    scaled_down_grad = 1.0 / math.sqrt(MODEL_WIDTH)
    scaled_up_grad = adapter_scale / math.sqrt(ADAPTER_RANK)
    table_position = slot_of_adapter[adapter_per_group].astype(jnp.int32)
    selected_down = down_table_rows[table_position].astype(jnp.float32)
    selected_up = up_table_rows[table_position].astype(jnp.float32)
    grouped_x = activations.reshape(GROUPS, GROUP, MODEL_WIDTH).astype(jnp.float32)
    grouped_dy = query_gradient.reshape(GROUPS, GROUP, QUERY_WIDTH).astype(jnp.float32)
    low = (jnp.einsum('gtd,grd->gtr', grouped_x, selected_down) * scaled_down_grad).astype(jnp.bfloat16)
    backward_result = (jnp.einsum('gtq,grq->gtr', grouped_dy, selected_up) * scaled_up_grad).astype(jnp.bfloat16)
    frozen_term = lax.dot_general(query_gradient, query_matrix, (((1,), (1,)), ((), ())), preferred_element_type=jnp.float32)
    adapter_term = jnp.einsum('ivo,ios->ivs', backward_result.astype(jnp.float32), selected_down).reshape(TOKEN_COUNT, MODEL_WIDTH) * scaled_down_grad
    token_gradient = frozen_term + adapter_term
    grad_a = jnp.einsum('gtr,gtd->grd', backward_result.astype(jnp.float32), grouped_x) * scaled_down_grad
    grad_b = jnp.einsum('gtr,gtq->grq', low.astype(jnp.float32), grouped_dy) * scaled_up_grad
    onehot = (table_position[:, None] == jnp.arange(ADAPTER_COUNT, dtype=jnp.int32)[None, :]).astype(jnp.float32)
    down_lookup = jnp.einsum('ga,grd->ard', onehot, grad_a, precision=lax.Precision.HIGHEST)
    up_lookup = jnp.einsum('ga,grq->arq', onehot, grad_b, precision=lax.Precision.HIGHEST)
    down_after_step = (down_table_rows.astype(jnp.float32) - learning_rate * down_lookup).astype(jnp.bfloat16)
    up_after_step = (up_table_rows.astype(jnp.float32) - learning_rate * up_lookup).astype(jnp.bfloat16)
    return (token_gradient, down_after_step, up_after_step)
```

```python
import math

import jax
import jax.numpy as jnp
from jax import lax
from jax.experimental import pallas as pl
from jax.experimental.pallas import tpu as pltpu
from jax.sharding import PartitionSpec as P

MODEL_WIDTH = 8192
RANK = 16
GROUP = 128
ADAPTER_SCALE = 0.25
LEARNING_RATE = 1.5
SCALE_DOWN = 1.0 / math.sqrt(MODEL_WIDTH)
SCALE_UP = ADAPTER_SCALE / math.sqrt(RANK)

SIDE = 4
DEPTH = 8
OWNERS = SIDE * SIDE

POWER_SHIFT = 19.0

MESH = pl.DeviceIdType.MESH
F32 = jnp.float32
BF16 = jnp.bfloat16
I32 = jnp.int32
HOPS = 7
TARGET = ((4, 3, 3, 2, 2, 1, 1), (4, 5, 5, 6, 6, 7, 7))
HALF = ((0, 1, 0, 1, 0, 1, 0), (1, 0, 1, 0, 1, 0, 1))
W_ORDER = (4, 3, 5, 2, 6, 1, 7, 0)


def encode(v):
    u = v * (2.0**POWER_SHIFT)
    return ((u * jnp.abs(u)) * (u * u)).astype(BF16)


def decode(code):
    w = code.astype(F32)
    root = jnp.exp2(jnp.log(jnp.abs(w)) * (0.25 / math.log(2.0)) - POWER_SHIFT)
    return jnp.where(w < 0, -root, root)


class Gather:
    def __init__(self, buf, send, recv, first, second, cut):
        self.buf, self.send, self.recv, self.first, self.second = buf, send, recv, first, second
        rows = buf.shape[1]
        self.parts = {"all": (0, rows), "a": (0, cut), "b": (cut, rows - cut)}
        self.copies = {}

    def go(self, number, device, source, target, part):
        begin, size = self.parts[part]
        copy = pltpu.make_async_remote_copy(
            src_ref=self.buf.at[source, pl.ds(begin, size)],
            dst_ref=self.buf.at[target, pl.ds(begin, size)],
            send_sem=self.send.at[number],
            recv_sem=self.recv.at[number],
            device_id=device,
            device_id_type=MESH,
        )
        copy.start()
        self.copies[number] = copy

    def wait(self, number):
        self.copies[number].wait_recv()

    def start(self):
        self.go(0, self.first(1), 0, 12, "all")
        self.go(1, self.first(-1), 0, 4, "all")

    def across(self, i):
        self.go(4 + 4 * i, self.second(1), 4 * i, 4 * i + 3, "all")
        self.go(5 + 4 * i, self.second(-1), 4 * i, 4 * i + 1, "all")

    def pass_first(self):
        self.wait(0)
        self.go(2, self.first(1), 12, 8, "a")
        self.wait(1)
        self.go(3, self.first(-1), 4, 8, "b")

    def end_first(self):
        self.wait(2)
        self.wait(3)

    def pass_second(self, i):
        self.wait(4 + 4 * i)
        self.go(6 + 4 * i, self.second(1), 4 * i + 3, 4 * i + 2, "a")
        self.wait(5 + 4 * i)
        self.go(7 + 4 * i, self.second(-1), 4 * i + 1, 4 * i + 2, "b")

    def end(self):
        for i in range(SIDE):
            self.wait(6 + 4 * i)
            self.wait(7 + 4 * i)

    def drain(self):
        for copy in self.copies.values():
            copy.wait_send()


def kernel(
    x_hbm,
    dy_hbm,
    w_hbm,
    down_hbm,
    up_hbm,
    adapter,
    slot_of,
    token_out,
    down_out,
    up_out,
    xv,
    dyv,
    wv,
    tab0,
    tab1,
    gr0,
    gr1,
    ids,
    z_in,
    z_out,
    part,
    own,
    rank_own,
    rank_pair,
    rank_chip,
    rank_in,
    rank_all,
    out0,
    out1,
    links_v,
    links_s,
    local_sem,
    pair_send,
    pair_recv,
    t0_send,
    t0_recv,
    t1_send,
    t1_recv,
    g0_send,
    g0_recv,
    g1_send,
    g1_recv,
    z_send,
    z_recv,
    r_send,
    r_recv,
    a_send,
    a_recv,
    i_send,
    i_recv,
):
    dp, tensor = lax.axis_index("dp"), lax.axis_index("tensor")
    x, y = lax.div(dp, SIDE), lax.rem(dp, SIDE)
    z, core = lax.div(tensor, 2), lax.rem(tensor, 2)
    tokens, width = own.shape
    half = tokens // 2
    groups = tokens // GROUP
    mate = (dp, z * 2 + 1 - core)

    def along_x(d):
        return (lax.rem(x + d + SIDE, SIDE) * SIDE + y, tensor)

    def along_y(d):
        return (x * SIDE + lax.rem(y + d + SIDE, SIDE), tensor)

    def chip_z(d):
        return lax.rem(z + d + DEPTH, DEPTH)

    def along_z(d):
        return (dp, chip_z(d) * 2 + core)

    def place0(owner):
        i = lax.rem(lax.div(owner, SIDE) - x + SIDE, SIDE)
        return i * SIDE + lax.rem(lax.rem(owner, SIDE) - y + SIDE, SIDE)

    def place1(owner):
        i = lax.rem(lax.rem(owner, SIDE) - y + SIDE, SIDE)
        return i * SIDE + lax.rem(lax.div(owner, SIDE) - x + SIDE, SIDE)

    def w_rows(rel, parity):
        begin = pl.multiple_of((chip_z(rel) * 2 + parity) * width, width)
        return w_hbm.at[pl.ds(begin, width)]

    loads = [
        pltpu.make_async_copy(down_hbm, tab0.at[0], local_sem.at[0]),
        pltpu.make_async_copy(up_hbm, tab1.at[0], local_sem.at[1]),
        pltpu.make_async_copy(dy_hbm, dyv.at[0], local_sem.at[2]),
        pltpu.make_async_copy(x_hbm, xv, local_sem.at[3]),
    ]
    w_loads = {rel: pltpu.make_async_copy(w_rows(rel, core), wv.at[0, rel], local_sem.at[4 + rel]) for rel in W_ORDER}
    for copy in loads:
        copy.start()
    for rel in W_ORDER:
        w_loads[rel].start()

    row = lax.broadcasted_iota(I32, (8, 128), 0)
    tile = jnp.full((8, 128), -1, I32)
    for g in range(groups):
        tile = jnp.where(row == g, slot_of[adapter[g]], tile)
    ids[dp] = tile

    barrier = pltpu.get_barrier_semaphore()
    pl.semaphore_signal(barrier, inc=1, device_id=mate, device_id_type=MESH)
    for k in range(1, DEPTH):
        pl.semaphore_signal(barrier, inc=1, device_id=along_z(k), device_id_type=MESH)
    for k in range(1, OWNERS):
        pl.semaphore_signal(barrier, inc=1, device_id=(lax.rem(dp + k, OWNERS), tensor), device_id_type=MESH)
    pl.semaphore_wait(barrier, DEPTH + OWNERS - 1)

    def to_mate(source, target, number):
        return pltpu.make_async_remote_copy(
            src_ref=source,
            dst_ref=target,
            send_sem=pair_send.at[number],
            recv_sem=pair_recv.at[number],
            device_id=mate,
            device_id_type=MESH,
        )

    dy_pair = to_mate(dy_hbm, dyv.at[1], 8)
    dy_pair.start()
    w_pair = {rel: to_mate(w_rows(rel, 1 - core), wv.at[1, rel], rel) for rel in W_ORDER}
    w_pair[4].start()

    tables = (
        Gather(tab0, t0_send, t0_recv, along_x, along_y, 2),
        Gather(tab1, t1_send, t1_recv, along_y, along_x, 2),
    )
    loads[0].wait()
    tables[0].start()
    loads[1].wait()
    tables[1].start()
    for table in tables:
        table.across(0)
    for rel in W_ORDER[1:]:
        w_pair[rel].start()

    def frozen(rel, begin, size):
        rows = pl.ds(begin, size)
        dims = (((1,), (1,)), ((), ()))
        first = lax.dot_general(dyv[0, rows], wv[0, rel], dims, preferred_element_type=F32)
        second = lax.dot_general(dyv[1, rows], wv[1, rel], dims, preferred_element_type=F32)
        return first + second

    def z_copy(way, k):
        return pltpu.make_async_remote_copy(
            src_ref=z_out.at[way, k],
            dst_ref=z_in.at[way, k],
            send_sem=z_send.at[way, k],
            recv_sem=z_recv.at[way, k],
            device_id=along_z(1 - 2 * way),
            device_id_type=MESH,
        )

    z_copies = {(way, k): z_copy(way, k) for way in range(2) for k in range(HOPS)}
    strip = 32
    have = set()

    def z_step(k):
        for way in range(2):
            rel = TARGET[way][k]
            if rel not in have:
                have.add(rel)
                w_loads[rel].wait()
                w_pair[rel].wait_recv()
            part[way] = frozen(rel, HALF[way][k] * half, half)
            if k >= 2:
                z_copies[way, k - 2].wait_recv()

            def move(n, carry):
                rows = pl.ds(pl.multiple_of(n * strip, strip), strip)
                v = part[way, rows]
                if k >= 2:
                    v = v + decode(z_in[way, k - 2, rows])
                z_out[way, k, rows] = encode(v)
                return carry

            lax.fori_loop(0, half // strip, move, 0)
            z_copies[way, k].start()

    def z_end(way, k):
        begin = HALF[way][k] * half
        z_copies[way, k].wait_recv()

        def move(n, carry):
            rows = pl.ds(pl.multiple_of(begin + n * strip, strip), strip)
            own[rows] = own[rows] + decode(z_in[way, k, pl.ds(pl.multiple_of(n * strip, strip), strip)])
            return carry

        lax.fori_loop(0, half // strip, move, 0)

    loads[2].wait()
    dy_pair.wait_recv()
    z_step(0)
    for table in tables:
        table.pass_first()
        table.across(3)
        table.across(1)

    def id_copy(k, place):
        return pltpu.make_async_remote_copy(
            src_ref=ids.at[dp],
            dst_ref=ids.at[place],
            send_sem=i_send.at[k],
            recv_sem=i_recv.at[k],
            device_id=(lax.rem(dp + k, OWNERS), tensor),
            device_id_type=MESH,
        )

    for k in range(1, OWNERS):
        id_copy(k, dp).start()
    for table in tables:
        table.end_first()
        table.across(2)
    for i in (0, 3):
        for table in tables:
            table.pass_second(i)
    z_step(1)
    for i in (1, 2):
        for table in tables:
            table.pass_second(i)
    for table in tables:
        table.end()

    loads[3].wait()
    slots = [slot_of[adapter[g]] for g in range(groups)]
    downs, ups = [], []
    for s in slots:
        owner, at = lax.div(s, 4), lax.rem(s, 4)
        downs.append((place0(owner), at))
        ups.append((place1(owner), at))
    for g in range(groups):
        rows = pl.ds(g * GROUP, GROUP)
        dims = (((1,), (1,)), ((), ()))
        low = lax.dot_general(tab0[downs[g]], xv[rows], dims, preferred_element_type=F32)
        back = lax.dot_general(tab1[ups[g]], dyv[0, rows], dims, preferred_element_type=F32)
        rank_own[4 * g : 4 * g + 2] = low.reshape(2, 8, GROUP)
        rank_own[4 * g + 2 : 4 * g + 4] = back.reshape(2, 8, GROUP)
    rank_mate = to_mate(rank_own, rank_pair, 9)
    rank_mate.start()
    rank_mate.wait_recv()
    rank_chip[...] = rank_own[...] + rank_pair[...]
    chunk = rank_own.shape[0] // DEPTH

    def rank_part(d):
        return pl.ds(chip_z(d) * chunk, chunk)

    r_copies, a_copies = [], []
    for k in range(1, DEPTH):
        copy = pltpu.make_async_remote_copy(
            src_ref=rank_chip.at[rank_part(k)],
            dst_ref=rank_in.at[k],
            send_sem=r_send.at[k],
            recv_sem=r_recv.at[k],
            device_id=along_z(k),
            device_id_type=MESH,
        )
        copy.start()
        r_copies.append(copy)
    total = rank_chip[rank_part(0)]
    for k in range(1, DEPTH):
        r_copies[k - 1].wait_recv()
        total = total + rank_in[k]
    rank_all[rank_part(0)] = total

    def a_copy(k, d):
        return pltpu.make_async_remote_copy(
            src_ref=rank_all.at[rank_part(0)],
            dst_ref=rank_all.at[rank_part(d)],
            send_sem=a_send.at[k],
            recv_sem=a_recv.at[k],
            device_id=along_z(k),
            device_id_type=MESH,
        )

    for k in range(1, DEPTH):
        copy = a_copy(k, 0)
        copy.start()
        a_copies.append(copy)
    z_step(2)
    for k in range(1, DEPTH):
        a_copy(k, -k).wait_recv()

    def low_of(g):
        return (rank_all[4 * g : 4 * g + 2].reshape(RANK, GROUP) * SCALE_DOWN).astype(BF16)

    def back_of(g):
        return (rank_all[4 * g + 2 : 4 * g + 4].reshape(RANK, GROUP) * SCALE_UP).astype(BF16)

    for g in range(groups):
        rows = pl.ds(g * GROUP, GROUP)
        gr0[0, g] = jnp.dot(back_of(g), xv[rows], preferred_element_type=F32) * SCALE_DOWN
        gr1[0, g] = jnp.dot(low_of(g), dyv[0, rows], preferred_element_type=F32) * SCALE_UP
    grads = (
        Gather(gr0, g0_send, g0_recv, along_x, along_y, groups // 2),
        Gather(gr1, g1_send, g1_recv, along_y, along_x, groups // 2),
    )
    for grad in grads:
        grad.start()
    for grad in grads:
        grad.across(0)
    z_step(3)

    have.add(0)
    w_loads[0].wait()
    w_pair[0].wait_recv()
    for g in range(groups):
        rows = pl.ds(g * GROUP, GROUP)
        term = lax.dot_general(back_of(g), tab0[downs[g]], (((0,), (0,)), ((), ())), preferred_element_type=F32)
        own[rows] = frozen(0, g * GROUP, GROUP) + term * SCALE_DOWN

    for k in range(1, OWNERS):
        id_copy(k, lax.rem(dp - k + OWNERS, OWNERS)).wait_recv()
    by_row = ids[...].reshape(OWNERS * 8, 128)
    by_column = by_row.T
    row = lax.broadcasted_iota(I32, by_row.shape, 0)
    column = lax.broadcasted_iota(I32, by_row.shape, 1)
    before = jnp.where((by_row == by_column) & (row < column), row, -1)
    last = jnp.where(by_row == column, row, -1)
    links_v[0:1] = jnp.max(before, axis=0, keepdims=True)
    links_v[1:2] = jnp.max(last, axis=0, keepdims=True)
    links = pltpu.make_async_copy(links_v, links_s, local_sem.at[12])
    links.start()

    for grad in grads:
        grad.pass_first()
        grad.across(3)
        grad.across(1)
    z_step(4)
    for grad in grads:
        grad.pass_second(0)
    for grad in grads:
        grad.end_first()
        grad.across(2)
    z_step(5)
    for grad in grads:
        grad.pass_second(3)
    for grad in grads:
        grad.pass_second(1)
    z_step(6)
    for grad in grads:
        grad.pass_second(2)
    for way in range(2):
        z_end(way, 5)
    for grad in grads:
        grad.end()
    for grad in grads:
        grad.drain()
    links.wait()

    def add_owner(d, carry):
        for g in range(groups):
            link = links_s[0, d * 8 + g]
            keep = jnp.where(link >= 0, 1.0, 0.0).astype(F32)
            link = jnp.maximum(link, 0)
            owner, at = lax.div(link, 8), lax.rem(link, 8)
            here = place0(d)
            gr0[here, g] = gr0[here, g] + keep * gr0[place0(owner), at]
            here = place1(d)
            gr1[here, g] = gr1[here, g] + keep * gr1[place1(owner), at]
        return carry

    lax.fori_loop(0, OWNERS, add_owner, 0)

    def step_slot(s, carry):
        link = links_s[1, s]
        keep = jnp.where(link >= 0, LEARNING_RATE, 0.0).astype(F32)
        link = jnp.maximum(link, 0)
        owner, at = lax.div(link, 8), lax.rem(link, 8)
        home, spot = lax.div(s, 4), lax.rem(s, 4)
        out0[s] = (tab0[place0(home), spot].astype(F32) - keep * gr0[place0(owner), at]).astype(BF16)
        out1[s] = (tab1[place1(home), spot].astype(F32) - keep * gr1[place1(owner), at]).astype(BF16)
        return carry

    lax.fori_loop(0, out0.shape[0], step_slot, 0)
    stores = [
        pltpu.make_async_copy(out0, down_out, local_sem.at[13]),
        pltpu.make_async_copy(out1, up_out, local_sem.at[14]),
    ]
    for copy in stores:
        copy.start()

    for way in range(2):
        z_end(way, 6)
        rows = pl.ds(HALF[way][6] * half, half)
        copy = pltpu.make_async_copy(own.at[rows], token_out.at[rows], local_sem.at[15 + way])
        copy.start()
        stores.append(copy)

    for copy in [dy_pair, rank_mate, *w_pair.values(), *z_copies.values(), *r_copies, *a_copies]:
        copy.wait_send()
    for k in range(1, OWNERS):
        id_copy(k, dp).wait_send()
    for table in tables:
        table.drain()
    for copy in stores:
        copy.wait()


def shards(x, dy, w, down, up, adapter, slot_of):
    tokens, width = x.shape
    owned, rank, _ = down.shape
    groups = adapter.shape[0]
    slots = owned * OWNERS
    tiles = groups * 4
    any_space = pl.BlockSpec(memory_space=pl.ANY)
    smem = pl.BlockSpec(memory_space=pltpu.SMEM)
    dma = pltpu.SemaphoreType.DMA
    vmem = pltpu.VMEM
    return pl.pallas_call(
        kernel,
        out_shape=(
            jax.ShapeDtypeStruct((tokens, width), F32),
            jax.ShapeDtypeStruct((slots, rank, width), BF16),
            jax.ShapeDtypeStruct((slots, rank, width), BF16),
        ),
        in_specs=[any_space] * 5 + [smem] * 2,
        out_specs=(any_space,) * 3,
        scratch_shapes=[
            vmem((tokens, width), BF16),
            vmem((2, tokens, width), BF16),
            vmem((2, DEPTH, width, width), BF16),
            vmem((OWNERS, owned, rank, width), BF16),
            vmem((OWNERS, owned, rank, width), BF16),
            vmem((OWNERS, groups, rank, width), F32),
            vmem((OWNERS, groups, rank, width), F32),
            vmem((OWNERS, 8, 128), I32),
            vmem((2, HOPS, tokens // 2, width), BF16),
            vmem((2, HOPS, tokens // 2, width), BF16),
            vmem((2, tokens // 2, width), F32),
            vmem((tokens, width), F32),
            vmem((tiles, 8, GROUP), F32),
            vmem((tiles, 8, GROUP), F32),
            vmem((tiles, 8, GROUP), F32),
            vmem((DEPTH, tiles // DEPTH, 8, GROUP), F32),
            vmem((tiles, 8, GROUP), F32),
            vmem((slots, rank, width), BF16),
            vmem((slots, rank, width), BF16),
            vmem((8, 128), I32),
            pltpu.SMEM((8, 128), I32),
            dma((17,)),
            dma((10,)),
            dma((10,)),
        ]
        + [dma((20,))] * 8
        + [dma((2, HOPS))] * 2
        + [dma((DEPTH,))] * 4
        + [dma((OWNERS,))] * 2,
        compiler_params=pltpu.CompilerParams(
            collective_id=0, has_side_effects=True, vmem_limit_bytes=56 * 1024 * 1024
        ),
        name="lora_step",
    )(x, dy, w, down, up, adapter, slot_of)


def solution(mesh):
    return jax.shard_map(
        shards,
        mesh=mesh,
        in_specs=(
            P("dp", "tensor"),
            P("dp", "tensor"),
            P(None, "tensor"),
            P("dp", None, "tensor"),
            P("dp", None, "tensor"),
            P("dp"),
            P(),
        ),
        out_specs=(P("dp", "tensor"), P(None, None, "tensor"), P(None, None, "tensor")),
        check_vma=False,
    )
```

```python
import math

import jax
import jax.numpy as jnp
from jax import lax
from jax.experimental import pallas as pl
from jax.experimental.pallas import tpu as pltpu
from jax.sharding import PartitionSpec as P

MODEL_WIDTH = 8192
RANK = 16
GROUP = 128
ADAPTER_SCALE = 0.25
LEARNING_RATE = 1.5
SCALE_DOWN = 1.0 / math.sqrt(MODEL_WIDTH)
SCALE_UP = ADAPTER_SCALE / math.sqrt(RANK)

SIDE = 4
DEPTH = 8
OWNERS = SIDE * SIDE

POWER_SHIFT = 19.0

MESH = pl.DeviceIdType.MESH
F32 = jnp.float32
BF16 = jnp.bfloat16
I32 = jnp.int32
HOPS = 7
TARGET = ((4, 3, 3, 2, 2, 1, 1), (4, 5, 5, 6, 6, 7, 7))
HALF = ((0, 1, 0, 1, 0, 1, 0), (1, 0, 1, 0, 1, 0, 1))
W_ORDER = (4, 3, 5, 2, 6, 1, 7, 0)


def encode(v):
    u = v * (2.0**POWER_SHIFT)
    return ((u * jnp.abs(u)) * (u * u)).astype(BF16)


def decode(code):
    w = code.astype(F32)
    root = jnp.exp2(jnp.log(jnp.abs(w)) * (0.25 / math.log(2.0)) - POWER_SHIFT)
    return jnp.where(w < 0, -root, root)


BLOCK_SHIFT = 7.8


def encode_block(v):
    most = jnp.maximum(jnp.max(jnp.max(jnp.abs(v), axis=0, keepdims=True), axis=1, keepdims=True), 1e-30)
    u = v * (2.0**BLOCK_SHIFT / most)
    u2 = u * u
    u4 = u2 * u2
    return (((u4 * u4) * u4) * (u2 * (u * jnp.abs(u)))).astype(BF16), most


def decode_block(code, most):
    w = code.astype(F32)
    root = jnp.exp2(jnp.log(jnp.abs(w)) * (0.0625 / math.log(2.0)) - BLOCK_SHIFT)
    return jnp.where(w < 0, -root, root) * jnp.concatenate([most] * (w.shape[1] // 128), axis=1)


class Gather:
    def __init__(self, buf, send, recv, first, second, cut):
        self.buf, self.send, self.recv, self.first, self.second = buf, send, recv, first, second
        rows = buf.shape[1]
        self.parts = {"all": (0, rows), "a": (0, cut), "b": (cut, rows - cut)}
        self.copies = {}

    def go(self, number, device, source, target, part):
        begin, size = self.parts[part]
        copy = pltpu.make_async_remote_copy(
            src_ref=self.buf.at[source, pl.ds(begin, size)],
            dst_ref=self.buf.at[target, pl.ds(begin, size)],
            send_sem=self.send.at[number],
            recv_sem=self.recv.at[number],
            device_id=device,
            device_id_type=MESH,
        )
        copy.start()
        self.copies[number] = copy

    def wait(self, number):
        self.copies[number].wait_recv()

    def start(self):
        self.go(0, self.first(1), 0, 12, "all")
        self.go(1, self.first(-1), 0, 4, "all")

    def across(self, i):
        self.go(4 + 4 * i, self.second(1), 4 * i, 4 * i + 3, "all")
        self.go(5 + 4 * i, self.second(-1), 4 * i, 4 * i + 1, "all")

    def pass_first(self):
        self.wait(0)
        self.go(2, self.first(1), 12, 8, "a")
        self.wait(1)
        self.go(3, self.first(-1), 4, 8, "b")

    def end_first(self):
        self.wait(2)
        self.wait(3)

    def pass_second(self, i):
        self.wait(4 + 4 * i)
        self.go(6 + 4 * i, self.second(1), 4 * i + 3, 4 * i + 2, "a")
        self.wait(5 + 4 * i)
        self.go(7 + 4 * i, self.second(-1), 4 * i + 1, 4 * i + 2, "b")

    def end(self):
        for i in range(SIDE):
            self.wait(6 + 4 * i)
            self.wait(7 + 4 * i)

    def drain(self):
        for copy in self.copies.values():
            copy.wait_send()


def kernel(
    x_hbm,
    dy_hbm,
    w_hbm,
    down_hbm,
    up_hbm,
    adapter,
    slot_of,
    own_out,
    last_out,
    down_out,
    up_out,
    xv,
    dyv,
    wv,
    tab0,
    tab1,
    code0,
    code1,
    most,
    sum0,
    sum1,
    ids,
    z_in,
    z_out,
    part,
    own,
    rank_own,
    rank_pair,
    rank_chip,
    rank_in,
    rank_all,
    out0,
    out1,
    links_v,
    links_s,
    local_sem,
    pair_send,
    pair_recv,
    t0_send,
    t0_recv,
    t1_send,
    t1_recv,
    g0_send,
    g0_recv,
    g1_send,
    g1_recv,
    z_send,
    z_recv,
    r_send,
    r_recv,
    a_send,
    a_recv,
    i_send,
    i_recv,
    m_send,
    m_recv,
):
    dp, tensor = lax.axis_index("dp"), lax.axis_index("tensor")
    x, y = lax.div(dp, SIDE), lax.rem(dp, SIDE)
    z, core = lax.div(tensor, 2), lax.rem(tensor, 2)
    tokens, width = own.shape
    half = tokens // 2
    groups = tokens // GROUP
    mate = (dp, z * 2 + 1 - core)

    def along_x(d):
        return (lax.rem(x + d + SIDE, SIDE) * SIDE + y, tensor)

    def along_y(d):
        return (x * SIDE + lax.rem(y + d + SIDE, SIDE), tensor)

    def chip_z(d):
        return lax.rem(z + d + DEPTH, DEPTH)

    def along_z(d):
        return (dp, chip_z(d) * 2 + core)

    def place0(owner):
        i = lax.rem(lax.div(owner, SIDE) - x + SIDE, SIDE)
        return i * SIDE + lax.rem(lax.rem(owner, SIDE) - y + SIDE, SIDE)

    def place1(owner):
        i = lax.rem(lax.rem(owner, SIDE) - y + SIDE, SIDE)
        return i * SIDE + lax.rem(lax.div(owner, SIDE) - x + SIDE, SIDE)

    def w_rows(rel, parity):
        begin = pl.multiple_of((chip_z(rel) * 2 + parity) * width, width)
        return w_hbm.at[pl.ds(begin, width)]

    loads = [
        pltpu.make_async_copy(down_hbm, tab0.at[0], local_sem.at[0]),
        pltpu.make_async_copy(up_hbm, tab1.at[0], local_sem.at[1]),
        pltpu.make_async_copy(dy_hbm, dyv.at[0], local_sem.at[2]),
        pltpu.make_async_copy(x_hbm, xv, local_sem.at[3]),
    ]
    w_loads = {rel: pltpu.make_async_copy(w_rows(rel, core), wv.at[0, rel], local_sem.at[4 + rel]) for rel in W_ORDER}
    w_loads[4].start()
    loads[2].start()
    loads[0].start()
    loads[1].start()
    loads[3].start()
    for rel in W_ORDER[1:]:
        w_loads[rel].start()

    row = lax.broadcasted_iota(I32, (8, 128), 0)
    tile = jnp.full((8, 128), -1, I32)
    for g in range(groups):
        tile = jnp.where(row == g, slot_of[adapter[g]], tile)
    ids[dp] = tile

    barrier = pltpu.get_barrier_semaphore()
    pl.semaphore_signal(barrier, inc=1, device_id=mate, device_id_type=MESH)
    for k in range(1, DEPTH):
        pl.semaphore_signal(barrier, inc=1, device_id=along_z(k), device_id_type=MESH)
    for k in range(1, OWNERS):
        pl.semaphore_signal(barrier, inc=1, device_id=(lax.rem(dp + k, OWNERS), tensor), device_id_type=MESH)
    pl.semaphore_wait(barrier, DEPTH + OWNERS - 1)

    def to_mate(source, target, number):
        return pltpu.make_async_remote_copy(
            src_ref=source,
            dst_ref=target,
            send_sem=pair_send.at[number],
            recv_sem=pair_recv.at[number],
            device_id=mate,
            device_id_type=MESH,
        )

    w_pair = {rel: to_mate(w_rows(rel, 1 - core), wv.at[1, rel], rel) for rel in W_ORDER}

    def send_w(rel):
        begin = (chip_z(rel) * 2 + 1 - core) * width
        for n in range(0, width, GROUP):
            source = w_hbm.at[pl.ds(pl.multiple_of(begin + n, GROUP), GROUP)]
            to_mate(source, wv.at[1, rel, pl.ds(n, GROUP)], rel).start()

    send_w(4)
    dy_pair = {}
    for c in range(half // GROUP):
        for begin in (c * GROUP, half + c * GROUP):
            rows = pl.ds(begin, GROUP)
            dy_pair[begin] = to_mate(dy_hbm.at[rows], dyv.at[1, rows], 10 + begin // GROUP)
            dy_pair[begin].start()

    tables = (
        Gather(tab0, t0_send, t0_recv, along_x, along_y, 2),
        Gather(tab1, t1_send, t1_recv, along_y, along_x, 2),
    )
    loads[0].wait()
    tables[0].start()
    loads[1].wait()
    tables[1].start()
    for table in tables:
        table.across(0)
    send_w(3)
    send_w(5)

    def frozen(rel, begin, size):
        rows = pl.ds(begin, size)
        dims = (((1,), (1,)), ((), ()))
        first = lax.dot_general(dyv[0, rows], wv[0, rel], dims, preferred_element_type=F32)
        second = lax.dot_general(dyv[1, rows], wv[1, rel], dims, preferred_element_type=F32)
        return first + second

    def z_copy(way, k, rows=pl.ds(0, half)):
        return pltpu.make_async_remote_copy(
            src_ref=z_out.at[way, k, rows],
            dst_ref=z_in.at[way, k, rows] if k < HOPS - 1 else last_out.at[way, rows],
            send_sem=z_send.at[way, k],
            recv_sem=z_recv.at[way, k],
            device_id=along_z(1 - 2 * way),
            device_id_type=MESH,
        )

    z_copies = {(way, k): z_copy(way, k) for way in range(2) for k in range(HOPS)}
    strip = 64
    have = set()

    def z_step(k):
        for way in range(2):
            rel = TARGET[way][k]
            if rel not in have:
                have.add(rel)
                w_loads[rel].wait()
                w_pair[rel].wait_recv()
            part[way] = frozen(rel, HALF[way][k] * half, half)
            if k >= 2:
                z_copies[way, k - 2].wait_recv()

            def move(n, carry):
                rows = pl.ds(pl.multiple_of(n * strip, strip), strip)
                v = part[way, rows]
                if k >= 2:
                    v = v + decode(z_in[way, k - 2, rows])
                z_out[way, k, rows] = encode(v)
                z_copy(way, k, rows).start()
                return carry

            lax.fori_loop(0, half // strip, move, 0)

    def z_end(way, k):
        begin = HALF[way][k] * half
        z_copies[way, k].wait_recv()

        def move(n, carry):
            rows = pl.ds(pl.multiple_of(begin + n * strip, strip), strip)
            own[rows] = own[rows] + decode(z_in[way, k, pl.ds(pl.multiple_of(n * strip, strip), strip)])
            return carry

        lax.fori_loop(0, half // strip, move, 0)

    loads[2].wait()
    w_loads[4].wait()
    w_pair[4].wait_recv()
    have.add(4)
    for c in range(half // GROUP):
        for way in range(2):
            begin = HALF[way][0] * half + c * GROUP
            dy_pair[begin].wait_recv()
            rows = pl.ds(c * GROUP, GROUP)
            z_out[way, 0, rows] = encode(frozen(4, begin, GROUP))
            for n in range(GROUP // strip):
                z_copy(way, 0, pl.ds(c * GROUP + n * strip, strip)).start()
    for table in tables:
        table.pass_first()
        table.across(3)
        table.across(1)

    def id_copy(k, place):
        return pltpu.make_async_remote_copy(
            src_ref=ids.at[dp],
            dst_ref=ids.at[place],
            send_sem=i_send.at[k],
            recv_sem=i_recv.at[k],
            device_id=(lax.rem(dp + k, OWNERS), tensor),
            device_id_type=MESH,
        )

    for k in range(1, OWNERS):
        id_copy(k, dp).start()
    z_step(1)
    for rel in (2, 6, 0):
        send_w(rel)
    for table in tables:
        table.end_first()
        table.across(2)
    for i in (0, 3):
        for table in tables:
            table.pass_second(i)
    z_step(2)
    for i in (1, 2):
        for table in tables:
            table.pass_second(i)
    w_loads[0].wait()
    w_pair[0].wait_recv()
    for way in range(2):
        own[pl.ds(way * half, half)] = frozen(0, way * half, half)
    for table in tables:
        table.end()
    for rel in (1, 7):
        send_w(rel)

    loads[3].wait()
    slots = [slot_of[adapter[g]] for g in range(groups)]
    downs, ups = [], []
    for s in slots:
        owner, at = lax.div(s, 4), lax.rem(s, 4)
        downs.append((place0(owner), at))
        ups.append((place1(owner), at))
    for g in range(groups):
        rows = pl.ds(g * GROUP, GROUP)
        dims = (((1,), (1,)), ((), ()))
        low = lax.dot_general(tab0[downs[g]], xv[rows], dims, preferred_element_type=F32)
        back = lax.dot_general(tab1[ups[g]], dyv[0, rows], dims, preferred_element_type=F32)
        rank_own[0, g] = low
        rank_own[1, g] = back
    rank_mate = to_mate(rank_own.at[1 - core], rank_pair, 8)
    rank_mate.start()
    rank_mate.wait_recv()
    rank_chip[...] = rank_own[core] + rank_pair[...]

    r_copies = []
    for k in range(1, DEPTH):
        copy = pltpu.make_async_remote_copy(
            src_ref=rank_chip.at[lax.rem(chip_z(k), groups)],
            dst_ref=rank_in.at[k],
            send_sem=r_send.at[k],
            recv_sem=r_recv.at[k],
            device_id=along_z(k),
            device_id_type=MESH,
        )
        copy.start()
        r_copies.append(copy)
    z_step(3)
    total = rank_chip[lax.rem(z, groups)]
    for k in range(1, DEPTH):
        r_copies[k - 1].wait_recv()
        total = total + rank_in[k]
    rank_all[core, z] = (total * jnp.where(core == 0, SCALE_DOWN, SCALE_UP).astype(F32)).astype(BF16)

    def a_copy(k, d):
        return pltpu.make_async_remote_copy(
            src_ref=rank_all.at[core, z],
            dst_ref=rank_all.at[core, chip_z(d)],
            send_sem=a_send.at[k],
            recv_sem=a_recv.at[k],
            device_id=along_z(k),
            device_id_type=MESH,
        )

    a_copies = [a_copy(k, 0) for k in range(1, DEPTH)]
    for copy in a_copies:
        copy.start()
    for k in range(1, OWNERS):
        id_copy(k, lax.rem(dp - k + OWNERS, OWNERS)).wait_recv()
    by_row = ids[...].reshape(OWNERS * 8, 128)
    by_column = by_row.T
    row = lax.broadcasted_iota(I32, by_row.shape, 0)
    column = lax.broadcasted_iota(I32, by_row.shape, 1)
    before = jnp.where((by_row == by_column) & (row < column), row, -1)
    last = jnp.where(by_row == column, row, -1)
    links_v[0:1] = jnp.max(before, axis=0, keepdims=True)
    links_v[1:2] = jnp.max(last, axis=0, keepdims=True)
    links = pltpu.make_async_copy(links_v, links_s, local_sem.at[12])
    links.start()

    for k in range(1, DEPTH):
        a_copy(k, -k).wait_recv()
    halves_out = to_mate(rank_all.at[core], rank_all.at[core], 9)
    halves_out.start()
    z_step(4)
    to_mate(rank_all.at[core], rank_all.at[1 - core], 9).wait_recv()

    def low_of(g):
        return rank_all[0, g]

    def back_of(g):
        return rank_all[1, g]

    row = lax.broadcasted_iota(I32, (8, 128), 0)
    most0, most1 = jnp.zeros((8, 128), F32), jnp.zeros((8, 128), F32)
    for g in range(groups):
        rows = pl.ds(g * GROUP, GROUP)
        code, high = encode_block(jnp.dot(back_of(g), xv[rows], preferred_element_type=F32) * SCALE_DOWN)
        code0[0, g] = code
        most0 = jnp.where(row == g, high, most0)
        code, high = encode_block(jnp.dot(low_of(g), dyv[0, rows], preferred_element_type=F32) * SCALE_UP)
        code1[0, g] = code
        most1 = jnp.where(row == g, high, most1)
    most[dp, 0:8] = most0
    most[dp, 8:16] = most1
    grads = (
        Gather(code0, g0_send, g0_recv, along_x, along_y, groups // 2),
        Gather(code1, g1_send, g1_recv, along_y, along_x, groups // 2),
    )
    for grad in grads:
        grad.start()
    for grad in grads:
        grad.across(0)

    def most_copy(k, place):
        return pltpu.make_async_remote_copy(
            src_ref=most.at[dp],
            dst_ref=most.at[place],
            send_sem=m_send.at[k],
            recv_sem=m_recv.at[k],
            device_id=(lax.rem(dp + k, OWNERS), tensor),
            device_id_type=MESH,
        )

    for k in range(1, OWNERS):
        most_copy(k, dp).start()
    for g in range(groups):
        rows = pl.ds(g * GROUP, GROUP)
        term = lax.dot_general(back_of(g), tab0[downs[g]], (((0,), (0,)), ((), ())), preferred_element_type=F32)
        own[rows] = own[rows] + term * SCALE_DOWN

    z_step(5)
    for grad in grads:
        grad.pass_first()
        grad.across(3)
        grad.across(1)
    for grad in grads:
        grad.pass_second(0)
    for grad in grads:
        grad.end_first()
        grad.across(2)
    for i in (3, 1):
        for grad in grads:
            grad.pass_second(i)
    z_step(6)
    for grad in grads:
        grad.pass_second(2)
    for grad in grads:
        grad.end()
    for k in range(1, OWNERS):
        most_copy(k, lax.rem(dp - k + OWNERS, OWNERS)).wait_recv()
    links.wait()

    def add_owner(d, carry):
        for g in range(groups):
            link = links_s[0, d * 8 + g]
            keep = jnp.where(link >= 0, 1.0, 0.0).astype(F32)
            link = jnp.maximum(link, 0)
            owner, at = lax.div(link, 8), lax.rem(link, 8)
            sum0[d, g] = decode_block(code0[place0(d), g], most[d, g : g + 1]) + keep * sum0[owner, at]
            sum1[d, g] = decode_block(code1[place1(d), g], most[d, 8 + g : 9 + g]) + keep * sum1[owner, at]
        return carry

    sum0[0, 0] = jnp.zeros(sum0.shape[2:], F32)
    sum1[0, 0] = jnp.zeros(sum1.shape[2:], F32)
    lax.fori_loop(0, OWNERS, add_owner, 0)

    def step_slot(s, carry):
        link = links_s[1, s]
        keep = jnp.where(link >= 0, LEARNING_RATE, 0.0).astype(F32)
        link = jnp.maximum(link, 0)
        owner, at = lax.div(link, 8), lax.rem(link, 8)
        home, spot = lax.div(s, 4), lax.rem(s, 4)
        out0[s] = (tab0[place0(home), spot].astype(F32) - keep * sum0[owner, at]).astype(BF16)
        out1[s] = (tab1[place1(home), spot].astype(F32) - keep * sum1[owner, at]).astype(BF16)
        return carry

    lax.fori_loop(0, out0.shape[0], step_slot, 0)
    stores = [
        pltpu.make_async_copy(out0, down_out, local_sem.at[13]),
        pltpu.make_async_copy(out1, up_out, local_sem.at[14]),
    ]
    for copy in stores:
        copy.start()
    for way in range(2):
        z_end(way, 5)
    stores.append(pltpu.make_async_copy(own, own_out, local_sem.at[15]))
    stores[-1].start()
    for way in range(2):
        z_copies[way, HOPS - 1].wait_recv()
    for copy in [*dy_pair.values(), rank_mate, halves_out, *w_pair.values(), *z_copies.values(), *r_copies, *a_copies]:
        copy.wait_send()
    for k in range(1, OWNERS):
        id_copy(k, dp).wait_send()
        most_copy(k, dp).wait_send()
    for gather in [*tables, *grads]:
        gather.drain()
    for copy in stores:
        copy.wait()


PIECES = 6
COPIES = 4


def finish_kernel(own_in, last_in, down_in, up_in, token_out, down_out, up_out, own, last, down, up, load_sem, store_sem):
    def pieces(array, count):
        size = array.shape[0] // count
        return [pl.ds(c * size, size) for c in range(count)]

    def load(j, source, target, count):
        copies = [
            pltpu.make_async_copy(source.at[rows], target.at[rows], load_sem.at[j, c])
            for c, rows in enumerate(pieces(target, count))
        ]
        for copy in copies:
            copy.start()
        return copies

    stores = []

    def store(j, c, source, target, rows):
        copy = pltpu.make_async_copy(source.at[rows], target.at[rows], store_sem.at[j, c])
        copy.start()
        stores.append(copy)

    tables = [(load(2, down_in, down, COPIES), down, down_out), (load(3, up_in, up, COPIES), up, up_out)]
    own_loads, last_loads = load(0, own_in, own, PIECES), load(1, last_in, last, PIECES)
    for j, (loads, held, target) in enumerate(tables):
        for c, rows in enumerate(pieces(held, COPIES)):
            loads[c].wait()
            store(1 + j, c, held, target, rows)
    for c, rows in enumerate(pieces(own, PIECES)):
        own_loads[c].wait()
        last_loads[c].wait()
        own[rows] = own[rows] + decode(last[rows])
        store(0, c, own, token_out, rows)
    for copy in stores:
        copy.wait()


def finish(own, last, down, up):
    any_space = pl.BlockSpec(memory_space=pl.ANY)
    dma = pltpu.SemaphoreType.DMA
    return pl.pallas_call(
        finish_kernel,
        out_shape=tuple(jax.ShapeDtypeStruct(a.shape, a.dtype) for a in (own, down, up)),
        in_specs=[any_space] * 4,
        out_specs=(any_space,) * 3,
        scratch_shapes=[
            pltpu.VMEM(own.shape, F32),
            pltpu.VMEM(last.shape, BF16),
            pltpu.VMEM(down.shape, BF16),
            pltpu.VMEM(up.shape, BF16),
            dma((4, PIECES)),
            dma((3, PIECES)),
        ],
        compiler_params=pltpu.CompilerParams(vmem_limit_bytes=56 * 1024 * 1024),
        name="finish",
    )(own, last, down, up)


def shards(x, dy, w, down, up, adapter, slot_of):
    tokens, width = x.shape
    owned, rank, _ = down.shape
    groups = adapter.shape[0]
    slots = owned * OWNERS
    any_space = pl.BlockSpec(memory_space=pl.ANY)
    smem = pl.BlockSpec(memory_space=pltpu.SMEM)
    dma = pltpu.SemaphoreType.DMA
    vmem = pltpu.VMEM
    own, last, stepped_down, stepped_up = pl.pallas_call(
        kernel,
        out_shape=(
            jax.ShapeDtypeStruct((tokens, width), F32),
            jax.ShapeDtypeStruct((2, tokens // 2, width), BF16),
            jax.ShapeDtypeStruct((slots, rank, width), BF16),
            jax.ShapeDtypeStruct((slots, rank, width), BF16),
        ),
        in_specs=[any_space] * 5 + [smem] * 2,
        out_specs=(any_space,) * 4,
        scratch_shapes=[
            vmem((tokens, width), BF16),
            vmem((2, tokens, width), BF16),
            vmem((2, DEPTH, width, width), BF16),
            vmem((OWNERS, owned, rank, width), BF16),
            vmem((OWNERS, owned, rank, width), BF16),
            vmem((OWNERS, groups, rank, width), BF16),
            vmem((OWNERS, groups, rank, width), BF16),
            vmem((OWNERS, 16, 128), F32),
            vmem((OWNERS, groups, rank, width), F32),
            vmem((OWNERS, groups, rank, width), F32),
            vmem((OWNERS, 8, 128), I32),
            vmem((2, HOPS, tokens // 2, width), BF16),
            vmem((2, HOPS, tokens // 2, width), BF16),
            vmem((2, tokens // 2, width), F32),
            vmem((tokens, width), F32),
            vmem((2, groups, RANK, GROUP), F32),
            vmem((groups, RANK, GROUP), F32),
            vmem((groups, RANK, GROUP), F32),
            vmem((DEPTH, RANK, GROUP), F32),
            vmem((2, DEPTH, RANK, GROUP), BF16),
            vmem((slots, rank, width), BF16),
            vmem((slots, rank, width), BF16),
            vmem((8, 128), I32),
            pltpu.SMEM((8, 128), I32),
            dma((16,)),
            dma((10 + groups,)),
            dma((10 + groups,)),
        ]
        + [dma((20,))] * 8
        + [dma((2, HOPS))] * 2
        + [dma((DEPTH,))] * 4
        + [dma((OWNERS,))] * 4,
        compiler_params=pltpu.CompilerParams(
            collective_id=0, has_side_effects=True, vmem_limit_bytes=56 * 1024 * 1024
        ),
        name="lora_step",
    )(x, dy, w, down, up, adapter, slot_of)
    return finish(own, last.reshape(tokens, width), stepped_down, stepped_up)


def solution(mesh):
    return jax.shard_map(
        shards,
        mesh=mesh,
        in_specs=(
            P("dp", "tensor"),
            P("dp", "tensor"),
            P(None, "tensor"),
            P("dp", None, "tensor"),
            P("dp", None, "tensor"),
            P("dp"),
            P(),
        ),
        out_specs=(P("dp", "tensor"), P(None, None, "tensor"), P(None, None, "tensor")),
        check_vma=False,
    )
```

```python
import math

import jax
import jax.numpy as jnp
from jax import lax
from jax.experimental import pallas as pl
from jax.experimental.pallas import tpu as pltpu
from jax.sharding import PartitionSpec as P

MODEL_WIDTH = 8192
RANK = 16
GROUP = 128
ADAPTER_SCALE = 0.25
LEARNING_RATE = 1.5
SCALE_DOWN = 1.0 / math.sqrt(MODEL_WIDTH)
SCALE_UP = ADAPTER_SCALE / math.sqrt(RANK)

SIDE = 4
DEPTH = 8
OWNERS = SIDE * SIDE

POWER_SHIFT = 19.0

MESH = pl.DeviceIdType.MESH
F32 = jnp.float32
BF16 = jnp.bfloat16
I32 = jnp.int32
HOPS = 7
TARGET = ((4, 3, 3, 2, 2, 1, 1), (4, 5, 5, 6, 6, 7, 7))
HALF = ((0, 1, 0, 1, 0, 1, 0), (1, 0, 1, 0, 1, 0, 1))
W_ORDER = (4, 3, 5, 2, 6, 1, 7, 0)


def encode(v):
    u = v * (2.0**POWER_SHIFT)
    return ((u * jnp.abs(u)) * (u * u)).astype(BF16)


def decode(code):
    w = code.astype(F32)
    root = jnp.exp2(jnp.log(jnp.abs(w)) * (0.25 / math.log(2.0)) - POWER_SHIFT)
    return jnp.where(w < 0, -root, root)


BLOCK_SHIFT = 7.8


def encode_block(v):
    most = jnp.maximum(jnp.max(jnp.max(jnp.abs(v), axis=0, keepdims=True), axis=1, keepdims=True), 1e-30)
    u = v * (2.0**BLOCK_SHIFT / most)
    u2 = u * u
    u4 = u2 * u2
    return (((u4 * u4) * u4) * (u2 * (u * jnp.abs(u)))).astype(BF16), most


def decode_block(code, most):
    w = code.astype(F32)
    root = jnp.exp2(jnp.log(jnp.abs(w)) * (0.0625 / math.log(2.0)) - BLOCK_SHIFT)
    return jnp.where(w < 0, -root, root) * jnp.concatenate([most] * (w.shape[1] // 128), axis=1)


class Gather:
    def __init__(self, buf, send, recv, first, second, cut):
        self.buf, self.send, self.recv, self.first, self.second = buf, send, recv, first, second
        rows = buf.shape[1]
        self.parts = {"all": (0, rows), "a": (0, cut), "b": (cut, rows - cut)}
        self.copies = {}

    def go(self, number, device, source, target, part):
        begin, size = self.parts[part]
        copy = pltpu.make_async_remote_copy(
            src_ref=self.buf.at[source, pl.ds(begin, size)],
            dst_ref=self.buf.at[target, pl.ds(begin, size)],
            send_sem=self.send.at[number],
            recv_sem=self.recv.at[number],
            device_id=device,
            device_id_type=MESH,
        )
        copy.start()
        self.copies[number] = copy

    def wait(self, number):
        self.copies[number].wait_recv()

    def start(self):
        self.go(0, self.first(1), 0, 12, "all")
        self.go(1, self.first(-1), 0, 4, "all")

    def across(self, i):
        self.go(4 + 4 * i, self.second(1), 4 * i, 4 * i + 3, "all")
        self.go(5 + 4 * i, self.second(-1), 4 * i, 4 * i + 1, "all")

    def pass_first(self):
        self.wait(0)
        self.go(2, self.first(1), 12, 8, "a")
        self.wait(1)
        self.go(3, self.first(-1), 4, 8, "b")

    def end_first(self):
        self.wait(2)
        self.wait(3)

    def pass_second(self, i):
        self.wait(4 + 4 * i)
        self.go(6 + 4 * i, self.second(1), 4 * i + 3, 4 * i + 2, "a")
        self.wait(5 + 4 * i)
        self.go(7 + 4 * i, self.second(-1), 4 * i + 1, 4 * i + 2, "b")

    def end(self):
        for i in range(SIDE):
            self.wait(6 + 4 * i)
            self.wait(7 + 4 * i)

    def drain(self):
        for copy in self.copies.values():
            copy.wait_send()


def kernel(
    x_hbm,
    dy_hbm,
    w_hbm,
    down_hbm,
    up_hbm,
    adapter_hbm,
    slot_of_hbm,
    own_out,
    last_out,
    down_out,
    up_out,
    xv,
    dyv,
    wv,
    tab0,
    tab1,
    code0,
    code1,
    most,
    sum0,
    sum1,
    ids,
    z_in,
    z_out,
    part,
    own,
    rank_own,
    rank_pair,
    rank_chip,
    rank_in,
    rank_all,
    out0,
    out1,
    links_v,
    links_s,
    adapter,
    slot_of,
    local_sem,
    pair_send,
    pair_recv,
    t0_send,
    t0_recv,
    t1_send,
    t1_recv,
    g0_send,
    g0_recv,
    g1_send,
    g1_recv,
    z_send,
    z_recv,
    r_send,
    r_recv,
    a_send,
    a_recv,
    i_send,
    i_recv,
    m_send,
    m_recv,
):
    dp, tensor = lax.axis_index("dp"), lax.axis_index("tensor")
    x, y = lax.div(dp, SIDE), lax.rem(dp, SIDE)
    z, core = lax.div(tensor, 2), lax.rem(tensor, 2)
    tokens, width = own.shape
    half = tokens // 2
    groups = tokens // GROUP
    mate = (dp, z * 2 + 1 - core)

    def along_x(d):
        return (lax.rem(x + d + SIDE, SIDE) * SIDE + y, tensor)

    def along_y(d):
        return (x * SIDE + lax.rem(y + d + SIDE, SIDE), tensor)

    def chip_z(d):
        return lax.rem(z + d + DEPTH, DEPTH)

    def along_z(d):
        return (dp, chip_z(d) * 2 + core)

    def place0(owner):
        i = lax.rem(lax.div(owner, SIDE) - x + SIDE, SIDE)
        return i * SIDE + lax.rem(lax.rem(owner, SIDE) - y + SIDE, SIDE)

    def place1(owner):
        i = lax.rem(lax.rem(owner, SIDE) - y + SIDE, SIDE)
        return i * SIDE + lax.rem(lax.div(owner, SIDE) - x + SIDE, SIDE)

    def w_rows(rel, parity):
        begin = pl.multiple_of((chip_z(rel) * 2 + parity) * width, width)
        return w_hbm.at[pl.ds(begin, width)]

    loads = [
        pltpu.make_async_copy(down_hbm, tab0.at[0], local_sem.at[0]),
        pltpu.make_async_copy(up_hbm, tab1.at[0], local_sem.at[1]),
        pltpu.make_async_copy(dy_hbm, dyv.at[0], local_sem.at[2]),
        pltpu.make_async_copy(x_hbm, xv, local_sem.at[3]),
    ]
    w_loads = {rel: pltpu.make_async_copy(w_rows(rel, core), wv.at[0, rel], local_sem.at[4 + rel]) for rel in W_ORDER}
    ids_loads = [
        pltpu.make_async_copy(adapter_hbm, adapter, local_sem.at[16]),
        pltpu.make_async_copy(slot_of_hbm, slot_of, local_sem.at[17]),
    ]
    for copy in ids_loads:
        copy.start()
    w_loads[4].start()
    loads[2].start()
    loads[0].start()
    loads[1].start()
    loads[3].start()
    for rel in W_ORDER[1:]:
        w_loads[rel].start()

    for copy in ids_loads:
        copy.wait()
    row = lax.broadcasted_iota(I32, (8, 128), 0)
    tile = jnp.full((8, 128), -1, I32)
    for g in range(groups):
        tile = jnp.where(row == g, slot_of[adapter[g]], tile)
    ids[dp] = tile

    barrier = pltpu.get_barrier_semaphore()
    pl.semaphore_signal(barrier, inc=1, device_id=mate, device_id_type=MESH)
    for k in range(1, DEPTH):
        pl.semaphore_signal(barrier, inc=1, device_id=along_z(k), device_id_type=MESH)
    for k in range(1, OWNERS):
        pl.semaphore_signal(barrier, inc=1, device_id=(lax.rem(dp + k, OWNERS), tensor), device_id_type=MESH)
    pl.semaphore_wait(barrier, DEPTH + OWNERS - 1)

    def to_mate(source, target, number):
        return pltpu.make_async_remote_copy(
            src_ref=source,
            dst_ref=target,
            send_sem=pair_send.at[number],
            recv_sem=pair_recv.at[number],
            device_id=mate,
            device_id_type=MESH,
        )

    w_pair = {rel: to_mate(w_rows(rel, 1 - core), wv.at[1, rel], rel) for rel in W_ORDER}

    def send_w(rel):
        begin = (chip_z(rel) * 2 + 1 - core) * width
        for n in range(0, width, GROUP):
            source = w_hbm.at[pl.ds(pl.multiple_of(begin + n, GROUP), GROUP)]
            to_mate(source, wv.at[1, rel, pl.ds(n, GROUP)], rel).start()

    send_w(4)
    dy_pair = {}
    for c in range(half // GROUP):
        for begin in (c * GROUP, half + c * GROUP):
            rows = pl.ds(begin, GROUP)
            dy_pair[begin] = to_mate(dy_hbm.at[rows], dyv.at[1, rows], 10 + begin // GROUP)
            dy_pair[begin].start()

    tables = (
        Gather(tab0, t0_send, t0_recv, along_x, along_y, 2),
        Gather(tab1, t1_send, t1_recv, along_y, along_x, 2),
    )
    send_w(3)
    send_w(5)

    def frozen(rel, begin, size):
        rows = pl.ds(begin, size)
        dims = (((1,), (1,)), ((), ()))
        first = lax.dot_general(dyv[0, rows], wv[0, rel], dims, preferred_element_type=F32)
        second = lax.dot_general(dyv[1, rows], wv[1, rel], dims, preferred_element_type=F32)
        return first + second

    pieces = half // GROUP

    def z_copy(way, m):
        k, rows = m // pieces, pl.ds(m % pieces * GROUP, GROUP)
        return pltpu.make_async_remote_copy(
            src_ref=z_out.at[way, k, rows],
            dst_ref=z_in.at[way, k, rows] if k < HOPS - 1 else last_out.at[way, rows],
            send_sem=z_send.at[way, m],
            recv_sem=z_recv.at[way, m],
            device_id=along_z(1 - 2 * way),
            device_id_type=MESH,
        )

    z_copies = {(way, m): z_copy(way, m) for way in range(2) for m in range(HOPS * pieces)}
    strip = 64
    have = set()

    def z_step(m):
        k, j = m // pieces, m % pieces
        for way in range(2):
            rel, begin = TARGET[way][k], HALF[way][k] * half + j * GROUP
            if rel not in have:
                have.add(rel)
                w_loads[rel].wait()
                w_pair[rel].wait_recv()
            if k == 0:
                dy_pair[begin].wait_recv()
            part[way] = frozen(rel, begin, GROUP)
            if k >= 2:
                z_copies[way, m - 2 * pieces].wait_recv()

            def move(n, carry):
                rows = pl.ds(pl.multiple_of(j * GROUP + n * strip, strip), strip)
                v = part[way, pl.ds(pl.multiple_of(n * strip, strip), strip)]
                if k >= 2:
                    v = v + decode(z_in[way, k - 2, rows])
                z_out[way, k, rows] = encode(v)
                return carry

            lax.fori_loop(0, GROUP // strip, move, 0)
            z_copies[way, m].start()

    def z_steps(first, last):
        for m in range(first, last + 1):
            z_step(m)

    def z_end(way, k):
        begin = HALF[way][k] * half
        for j in range(pieces):
            z_copies[way, k * pieces + j].wait_recv()

        def move(n, carry):
            rows = pl.ds(pl.multiple_of(begin + n * strip, strip), strip)
            own[rows] = own[rows] + decode(z_in[way, k, pl.ds(pl.multiple_of(n * strip, strip), strip)])
            return carry

        lax.fori_loop(0, half // strip, move, 0)

    loads[2].wait()
    z_step(0)
    loads[0].wait()
    tables[0].start()
    loads[1].wait()
    tables[1].start()
    for table in tables:
        table.across(0)
    z_steps(1, 2)
    for table in tables:
        table.pass_first()
        table.across(3)
        table.across(1)

    def id_copy(k, place):
        return pltpu.make_async_remote_copy(
            src_ref=ids.at[dp],
            dst_ref=ids.at[place],
            send_sem=i_send.at[k],
            recv_sem=i_recv.at[k],
            device_id=(lax.rem(dp + k, OWNERS), tensor),
            device_id_type=MESH,
        )

    for k in range(1, OWNERS):
        id_copy(k, dp).start()
    z_steps(3, 5)
    for rel in (2, 6, 0):
        send_w(rel)
    for table in tables:
        table.end_first()
        table.across(2)
    for i in (0, 3, 1, 2):
        for table in tables:
            table.pass_second(i)
    w_loads[0].wait()
    w_pair[0].wait_recv()
    for way in range(2):
        own[pl.ds(way * half, half)] = frozen(0, way * half, half)
    z_steps(6, 7)
    for table in tables:
        table.end()
    for rel in (1, 7):
        send_w(rel)

    loads[3].wait()
    slots = [slot_of[adapter[g]] for g in range(groups)]
    downs, ups = [], []
    for s in slots:
        owner, at = lax.div(s, 4), lax.rem(s, 4)
        downs.append((place0(owner), at))
        ups.append((place1(owner), at))
    for g in range(groups):
        rows = pl.ds(g * GROUP, GROUP)
        dims = (((1,), (1,)), ((), ()))
        low = lax.dot_general(tab0[downs[g]], xv[rows], dims, preferred_element_type=F32)
        back = lax.dot_general(tab1[ups[g]], dyv[0, rows], dims, preferred_element_type=F32)
        rank_own[0, g] = low
        rank_own[1, g] = back
    rank_mate = to_mate(rank_own.at[1 - core], rank_pair, 8)
    rank_mate.start()
    rank_mate.wait_recv()
    rank_chip[...] = rank_own[core] + rank_pair[...]

    r_copies = []
    for k in range(1, DEPTH):
        copy = pltpu.make_async_remote_copy(
            src_ref=rank_chip.at[lax.rem(chip_z(k), groups)],
            dst_ref=rank_in.at[k],
            send_sem=r_send.at[k],
            recv_sem=r_recv.at[k],
            device_id=along_z(k),
            device_id_type=MESH,
        )
        copy.start()
        r_copies.append(copy)
    z_steps(8, 9)
    total = rank_chip[lax.rem(z, groups)]
    for k in range(1, DEPTH):
        r_copies[k - 1].wait_recv()
        total = total + rank_in[k]
    rank_all[core, z] = (total * jnp.where(core == 0, SCALE_DOWN, SCALE_UP).astype(F32)).astype(BF16)

    def a_copy(k, d):
        return pltpu.make_async_remote_copy(
            src_ref=rank_all.at[core, z],
            dst_ref=rank_all.at[core, chip_z(d)],
            send_sem=a_send.at[k],
            recv_sem=a_recv.at[k],
            device_id=along_z(k),
            device_id_type=MESH,
        )

    a_copies = [a_copy(k, 0) for k in range(1, DEPTH)]
    for copy in a_copies:
        copy.start()
    for k in range(1, OWNERS):
        id_copy(k, lax.rem(dp - k + OWNERS, OWNERS)).wait_recv()
    by_row = ids[...].reshape(OWNERS * 8, 128)
    by_column = by_row.T
    row = lax.broadcasted_iota(I32, by_row.shape, 0)
    column = lax.broadcasted_iota(I32, by_row.shape, 1)
    before = jnp.where((by_row == by_column) & (row < column), row, -1)
    last = jnp.where(by_row == column, row, -1)
    links_v[0:1] = jnp.max(before, axis=0, keepdims=True)
    links_v[1:2] = jnp.max(last, axis=0, keepdims=True)
    links = pltpu.make_async_copy(links_v, links_s, local_sem.at[12])
    links.start()

    z_steps(10, 13)
    for k in range(1, DEPTH):
        a_copy(k, -k).wait_recv()
    halves_out = to_mate(rank_all.at[core], rank_all.at[core], 9)
    halves_out.start()
    to_mate(rank_all.at[core], rank_all.at[1 - core], 9).wait_recv()

    def low_of(g):
        return rank_all[0, g]

    def back_of(g):
        return rank_all[1, g]

    row = lax.broadcasted_iota(I32, (8, 128), 0)
    most0, most1 = jnp.zeros((8, 128), F32), jnp.zeros((8, 128), F32)
    for g in range(groups):
        rows = pl.ds(g * GROUP, GROUP)
        code, high = encode_block(jnp.dot(back_of(g), xv[rows], preferred_element_type=F32) * SCALE_DOWN)
        code0[0, g] = code
        most0 = jnp.where(row == g, high, most0)
        code, high = encode_block(jnp.dot(low_of(g), dyv[0, rows], preferred_element_type=F32) * SCALE_UP)
        code1[0, g] = code
        most1 = jnp.where(row == g, high, most1)
    most[dp, 0:8] = most0
    most[dp, 8:16] = most1
    grads = (
        Gather(code0, g0_send, g0_recv, along_x, along_y, groups // 2),
        Gather(code1, g1_send, g1_recv, along_y, along_x, groups // 2),
    )
    for grad in grads:
        grad.start()
    for grad in grads:
        grad.across(0)

    def most_copy(k, place):
        return pltpu.make_async_remote_copy(
            src_ref=most.at[dp],
            dst_ref=most.at[place],
            send_sem=m_send.at[k],
            recv_sem=m_recv.at[k],
            device_id=(lax.rem(dp + k, OWNERS), tensor),
            device_id_type=MESH,
        )

    for k in range(1, OWNERS):
        most_copy(k, dp).start()
    for g in range(groups):
        rows = pl.ds(g * GROUP, GROUP)
        term = lax.dot_general(back_of(g), tab0[downs[g]], (((0,), (0,)), ((), ())), preferred_element_type=F32)
        own[rows] = own[rows] + term * SCALE_DOWN

    z_steps(14, 15)
    for grad in grads:
        grad.pass_first()
        grad.across(3)
        grad.across(1)
    z_step(16)
    for grad in grads:
        grad.pass_second(0)
    for grad in grads:
        grad.end_first()
        grad.across(2)
    z_step(17)
    for grad in grads:
        grad.pass_second(3)
    z_step(18)
    for grad in grads:
        grad.pass_second(1)
    z_step(19)
    for grad in grads:
        grad.pass_second(2)
    z_step(20)
    for grad in grads:
        grad.end()
    for k in range(1, OWNERS):
        most_copy(k, lax.rem(dp - k + OWNERS, OWNERS)).wait_recv()
    links.wait()

    def add_owner(d, carry):
        for g in range(groups):
            link = links_s[0, d * 8 + g]
            keep = jnp.where(link >= 0, 1.0, 0.0).astype(F32)
            link = jnp.maximum(link, 0)
            owner, at = lax.div(link, 8), lax.rem(link, 8)
            sum0[d, g] = decode_block(code0[place0(d), g], most[d, g : g + 1]) + keep * sum0[owner, at]
            sum1[d, g] = decode_block(code1[place1(d), g], most[d, 8 + g : 9 + g]) + keep * sum1[owner, at]
        return carry

    sum0[0, 0] = jnp.zeros(sum0.shape[2:], F32)
    sum1[0, 0] = jnp.zeros(sum1.shape[2:], F32)
    lax.fori_loop(0, OWNERS, add_owner, 0)

    def step_slot(s, carry):
        link = links_s[1, s]
        keep = jnp.where(link >= 0, LEARNING_RATE, 0.0).astype(F32)
        link = jnp.maximum(link, 0)
        owner, at = lax.div(link, 8), lax.rem(link, 8)
        home, spot = lax.div(s, 4), lax.rem(s, 4)
        out0[s] = (tab0[place0(home), spot].astype(F32) - keep * sum0[owner, at]).astype(BF16)
        out1[s] = (tab1[place1(home), spot].astype(F32) - keep * sum1[owner, at]).astype(BF16)
        return carry

    lax.fori_loop(0, out0.shape[0], step_slot, 0)
    stores = [
        pltpu.make_async_copy(out0, down_out, local_sem.at[13]),
        pltpu.make_async_copy(out1, up_out, local_sem.at[14]),
    ]
    for copy in stores:
        copy.start()
    for way in range(2):
        z_end(way, 5)
    stores.append(pltpu.make_async_copy(own, own_out, local_sem.at[15]))
    stores[-1].start()
    for way in range(2):
        for j in range(pieces):
            z_copies[way, (HOPS - 1) * pieces + j].wait_recv()
    for copy in [*dy_pair.values(), rank_mate, halves_out, *w_pair.values(), *z_copies.values(), *r_copies, *a_copies]:
        copy.wait_send()
    for k in range(1, OWNERS):
        id_copy(k, dp).wait_send()
        most_copy(k, dp).wait_send()
    for gather in [*tables, *grads]:
        gather.drain()
    for copy in stores:
        copy.wait()


PIECES = 6


def finish_kernel(own, last, down, up, token_out, down_out, up_out, total, sem):
    stores = [
        pltpu.make_async_copy(down, down_out, sem.at[PIECES]),
        pltpu.make_async_copy(up, up_out, sem.at[PIECES + 1]),
    ]
    for copy in stores:
        copy.start()
    size = total.shape[0] // PIECES
    for c in range(PIECES):
        rows = pl.ds(c * size, size)
        total[rows] = own[rows] + decode(last[rows])
        copy = pltpu.make_async_copy(total.at[rows], token_out.at[rows], sem.at[c])
        copy.start()
        stores.append(copy)
    for copy in stores:
        copy.wait()


def finish(own, last, down, up):
    any_space = pl.BlockSpec(memory_space=pl.ANY)
    return pl.pallas_call(
        finish_kernel,
        out_shape=tuple(jax.ShapeDtypeStruct(a.shape, a.dtype) for a in (own, down, up)),
        in_specs=[pl.BlockSpec(memory_space=pltpu.VMEM)] * 4,
        out_specs=(any_space,) * 3,
        scratch_shapes=[pltpu.VMEM(own.shape, F32), pltpu.SemaphoreType.DMA((PIECES + 2,))],
        compiler_params=pltpu.CompilerParams(vmem_limit_bytes=16 * 1024 * 1024),
        name="finish",
    )(own, last, down, up)


def shards(x, dy, w, down, up, adapter, slot_of):
    tokens, width = x.shape
    owned, rank, _ = down.shape
    groups = adapter.shape[0]
    slots = owned * OWNERS
    any_space = pl.BlockSpec(memory_space=pl.ANY)
    dma = pltpu.SemaphoreType.DMA
    vmem = pltpu.VMEM
    own, last, stepped_down, stepped_up = pl.pallas_call(
        kernel,
        out_shape=(
            vmem((tokens, width), F32),
            vmem((2, tokens // 2, width), BF16),
            vmem((slots, rank, width), BF16),
            vmem((slots, rank, width), BF16),
        ),
        in_specs=[pl.BlockSpec(memory_space=pltpu.HBM)] * 7,
        out_specs=(any_space,) * 4,
        scratch_shapes=[
            vmem((tokens, width), BF16),
            vmem((2, tokens, width), BF16),
            vmem((2, DEPTH, width, width), BF16),
            vmem((OWNERS, owned, rank, width), BF16),
            vmem((OWNERS, owned, rank, width), BF16),
            vmem((OWNERS, groups, rank, width), BF16),
            vmem((OWNERS, groups, rank, width), BF16),
            vmem((OWNERS, 16, 128), F32),
            vmem((OWNERS, groups, rank, width), F32),
            vmem((OWNERS, groups, rank, width), F32),
            vmem((OWNERS, 8, 128), I32),
            vmem((2, HOPS, tokens // 2, width), BF16),
            vmem((2, HOPS, tokens // 2, width), BF16),
            vmem((2, GROUP, width), F32),
            vmem((tokens, width), F32),
            vmem((2, groups, RANK, GROUP), F32),
            vmem((groups, RANK, GROUP), F32),
            vmem((groups, RANK, GROUP), F32),
            vmem((DEPTH, RANK, GROUP), F32),
            vmem((2, DEPTH, RANK, GROUP), BF16),
            vmem((slots, rank, width), BF16),
            vmem((slots, rank, width), BF16),
            vmem((8, 128), I32),
            pltpu.SMEM((8, 128), I32),
            pltpu.SMEM(adapter.shape, I32),
            pltpu.SMEM(slot_of.shape, I32),
            dma((18,)),
            dma((10 + groups,)),
            dma((10 + groups,)),
        ]
        + [dma((20,))] * 8
        + [dma((2, HOPS * (tokens // 2 // GROUP)))] * 2
        + [dma((DEPTH,))] * 4
        + [dma((OWNERS,))] * 4,
        compiler_params=pltpu.CompilerParams(
            collective_id=0, has_side_effects=True, vmem_limit_bytes=51 * 1024 * 1024
        ),
        name="lora_step",
    )(x, dy, w, down, up, adapter, slot_of)
    return finish(own, last.reshape(tokens, width), stepped_down, stepped_up)


def solution(mesh):
    return jax.shard_map(
        shards,
        mesh=mesh,
        in_specs=(
            P("dp", "tensor"),
            P("dp", "tensor"),
            P(None, "tensor"),
            P("dp", None, "tensor"),
            P("dp", None, "tensor"),
            P("dp"),
            P(),
        ),
        out_specs=(P("dp", "tensor"), P(None, None, "tensor"), P(None, None, "tensor")),
        check_vma=False,
    )
```

```python
import math

import jax
import jax.numpy as jnp
from jax import lax
from jax.experimental import pallas as pl
from jax.experimental.pallas import tpu as pltpu
from jax.sharding import PartitionSpec as P

MODEL_WIDTH = 8192
RANK = 16
GROUP = 128
ADAPTER_SCALE = 0.25
LEARNING_RATE = 1.5
SCALE_DOWN = 1.0 / math.sqrt(MODEL_WIDTH)
SCALE_UP = ADAPTER_SCALE / math.sqrt(RANK)

SIDE = 4
DEPTH = 8
OWNERS = SIDE * SIDE

POWER_SHIFT = 19.0

MESH = pl.DeviceIdType.MESH
F32 = jnp.float32
BF16 = jnp.bfloat16
I32 = jnp.int32
HOPS = 7
TARGET = ((4, 3, 3, 2, 2, 1, 1), (4, 5, 5, 6, 6, 7, 7))
HALF = ((0, 1, 0, 1, 0, 1, 0), (1, 0, 1, 0, 1, 0, 1))
W_ORDER = (4, 3, 5, 2, 6, 1, 7, 0)


def encode(v):
    u = v * (2.0**POWER_SHIFT)
    return ((u * jnp.abs(u)) * (u * u)).astype(BF16)


def decode(code):
    w = code.astype(F32)
    root = jnp.exp2(jnp.log(jnp.abs(w)) * (0.25 / math.log(2.0)) - POWER_SHIFT)
    return jnp.where(w < 0, -root, root)


BLOCK_SHIFT = 7.8


def encode_block(v):
    most = jnp.maximum(jnp.max(jnp.max(jnp.abs(v), axis=0, keepdims=True), axis=1, keepdims=True), 1e-30)
    u = v * (2.0**BLOCK_SHIFT / most)
    u2 = u * u
    u4 = u2 * u2
    return (((u4 * u4) * u4) * (u2 * (u * jnp.abs(u)))).astype(BF16), most


def decode_block(code, most):
    w = code.astype(F32)
    root = jnp.exp2(jnp.log(jnp.abs(w)) * (0.0625 / math.log(2.0)) - BLOCK_SHIFT)
    return jnp.where(w < 0, -root, root) * jnp.concatenate([most] * (w.shape[1] // 128), axis=1)


class Gather:
    def __init__(self, buf, send, recv, first, second, cut):
        self.buf, self.send, self.recv, self.first, self.second = buf, send, recv, first, second
        rows = buf.shape[1]
        self.parts = {"all": (0, rows), "a": (0, cut), "b": (cut, rows - cut)}
        self.copies = {}

    def go(self, number, device, source, target, part):
        begin, size = self.parts[part]
        copy = pltpu.make_async_remote_copy(
            src_ref=self.buf.at[source, pl.ds(begin, size)],
            dst_ref=self.buf.at[target, pl.ds(begin, size)],
            send_sem=self.send.at[number],
            recv_sem=self.recv.at[number],
            device_id=device,
            device_id_type=MESH,
        )
        copy.start()
        self.copies[number] = copy

    def wait(self, number):
        self.copies[number].wait_recv()

    def start(self):
        self.go(0, self.first(1), 0, 12, "all")
        self.go(1, self.first(-1), 0, 4, "all")

    def across(self, i):
        self.go(4 + 4 * i, self.second(1), 4 * i, 4 * i + 3, "all")
        self.go(5 + 4 * i, self.second(-1), 4 * i, 4 * i + 1, "all")

    def pass_first(self):
        self.wait(0)
        self.go(2, self.first(1), 12, 8, "a")
        self.wait(1)
        self.go(3, self.first(-1), 4, 8, "b")

    def end_first(self):
        self.wait(2)
        self.wait(3)

    def pass_second(self, i):
        self.wait(4 + 4 * i)
        self.go(6 + 4 * i, self.second(1), 4 * i + 3, 4 * i + 2, "a")
        self.wait(5 + 4 * i)
        self.go(7 + 4 * i, self.second(-1), 4 * i + 1, 4 * i + 2, "b")

    def end(self):
        for i in range(SIDE):
            self.wait(6 + 4 * i)
            self.wait(7 + 4 * i)

    def drain(self):
        for copy in self.copies.values():
            copy.wait_send()


def kernel(
    x_hbm,
    dy_hbm,
    w_hbm,
    down_hbm,
    up_hbm,
    adapter_hbm,
    slot_of_hbm,
    own_out,
    last_out,
    down_out,
    up_out,
    xv,
    dyv,
    wv,
    tab0,
    tab1,
    code0,
    code1,
    most,
    sum0,
    sum1,
    ids,
    z_in,
    z_out,
    part,
    own,
    rank_own,
    rank_pair,
    rank_chip,
    rank_in,
    rank_all,
    out0,
    out1,
    links_v,
    links_s,
    adapter,
    slot_of,
    local_sem,
    pair_send,
    pair_recv,
    t0_send,
    t0_recv,
    t1_send,
    t1_recv,
    g0_send,
    g0_recv,
    g1_send,
    g1_recv,
    z_send,
    z_recv,
    r_send,
    r_recv,
    a_send,
    a_recv,
    i_send,
    i_recv,
    m_send,
    m_recv,
):
    dp, tensor = lax.axis_index("dp"), lax.axis_index("tensor")
    x, y = lax.div(dp, SIDE), lax.rem(dp, SIDE)
    z, core = lax.div(tensor, 2), lax.rem(tensor, 2)
    tokens, width = own.shape
    half = tokens // 2
    groups = tokens // GROUP
    mate = (dp, z * 2 + 1 - core)

    def along_x(d):
        return (lax.rem(x + d + SIDE, SIDE) * SIDE + y, tensor)

    def along_y(d):
        return (x * SIDE + lax.rem(y + d + SIDE, SIDE), tensor)

    def chip_z(d):
        return lax.rem(z + d + DEPTH, DEPTH)

    def along_z(d):
        return (dp, chip_z(d) * 2 + core)

    def place0(owner):
        i = lax.rem(lax.div(owner, SIDE) - x + SIDE, SIDE)
        return i * SIDE + lax.rem(lax.rem(owner, SIDE) - y + SIDE, SIDE)

    def place1(owner):
        i = lax.rem(lax.rem(owner, SIDE) - y + SIDE, SIDE)
        return i * SIDE + lax.rem(lax.div(owner, SIDE) - x + SIDE, SIDE)

    def w_rows(rel, parity):
        begin = pl.multiple_of((chip_z(rel) * 2 + parity) * width, width)
        return w_hbm.at[pl.ds(begin, width)]

    loads = [
        pltpu.make_async_copy(down_hbm, tab0.at[0], local_sem.at[0]),
        pltpu.make_async_copy(up_hbm, tab1.at[0], local_sem.at[1]),
        pltpu.make_async_copy(dy_hbm, dyv.at[0], local_sem.at[2]),
        pltpu.make_async_copy(x_hbm, xv, local_sem.at[3]),
    ]
    w_loads = {rel: pltpu.make_async_copy(w_rows(rel, core), wv.at[0, rel], local_sem.at[4 + rel]) for rel in W_ORDER}
    ids_loads = [
        pltpu.make_async_copy(adapter_hbm, adapter, local_sem.at[16]),
        pltpu.make_async_copy(slot_of_hbm, slot_of, local_sem.at[17]),
    ]
    for copy in ids_loads:
        copy.start()
    w_loads[4].start()
    loads[2].start()
    loads[0].start()
    loads[1].start()
    loads[3].start()
    for rel in W_ORDER[1:]:
        w_loads[rel].start()

    for copy in ids_loads:
        copy.wait()
    row = lax.broadcasted_iota(I32, (8, 128), 0)
    tile = jnp.full((8, 128), -1, I32)
    for g in range(groups):
        tile = jnp.where(row == g, slot_of[adapter[g]], tile)
    ids[dp] = tile

    barrier = pltpu.get_barrier_semaphore()
    pl.semaphore_signal(barrier, inc=1, device_id=mate, device_id_type=MESH)
    for k in range(1, DEPTH):
        pl.semaphore_signal(barrier, inc=1, device_id=along_z(k), device_id_type=MESH)
    for k in range(1, OWNERS):
        pl.semaphore_signal(barrier, inc=1, device_id=(lax.rem(dp + k, OWNERS), tensor), device_id_type=MESH)
    pl.semaphore_wait(barrier, DEPTH + OWNERS - 1)

    def to_mate(source, target, number):
        return pltpu.make_async_remote_copy(
            src_ref=source,
            dst_ref=target,
            send_sem=pair_send.at[number],
            recv_sem=pair_recv.at[number],
            device_id=mate,
            device_id_type=MESH,
        )

    w_pair = {rel: to_mate(w_rows(rel, 1 - core), wv.at[1, rel], rel) for rel in W_ORDER}

    def send_w(rel):
        begin = (chip_z(rel) * 2 + 1 - core) * width
        for n in range(0, width, GROUP):
            source = w_hbm.at[pl.ds(pl.multiple_of(begin + n, GROUP), GROUP)]
            to_mate(source, wv.at[1, rel, pl.ds(n, GROUP)], rel).start()

    send_w(4)
    dy_pair = {}
    for c in range(half // GROUP):
        for begin in (c * GROUP, half + c * GROUP):
            rows = pl.ds(begin, GROUP)
            dy_pair[begin] = to_mate(dy_hbm.at[rows], dyv.at[1, rows], 10 + begin // GROUP)
            dy_pair[begin].start()

    tables = (
        Gather(tab0, t0_send, t0_recv, along_x, along_y, 2),
        Gather(tab1, t1_send, t1_recv, along_y, along_x, 2),
    )
    send_w(3)
    send_w(5)

    def frozen(rel, begin, size):
        rows = pl.ds(begin, size)
        dims = (((1,), (1,)), ((), ()))
        first = lax.dot_general(dyv[0, rows], wv[0, rel], dims, preferred_element_type=F32)
        second = lax.dot_general(dyv[1, rows], wv[1, rel], dims, preferred_element_type=F32)
        return first + second

    pieces = half // GROUP

    def z_copy(way, m):
        k, rows = m // pieces, pl.ds(m % pieces * GROUP, GROUP)
        return pltpu.make_async_remote_copy(
            src_ref=z_out.at[way, k, rows],
            dst_ref=z_in.at[way, k, rows] if k < HOPS - 1 else last_out.at[way, rows],
            send_sem=z_send.at[way, m],
            recv_sem=z_recv.at[way, m],
            device_id=along_z(1 - 2 * way),
            device_id_type=MESH,
        )

    z_copies = {(way, m): z_copy(way, m) for way in range(2) for m in range(HOPS * pieces)}
    strip = 64
    have = set()

    def z_step(m):
        k, j = m // pieces, m % pieces
        for way in range(2):
            rel, begin = TARGET[way][k], HALF[way][k] * half + j * GROUP
            if rel not in have:
                have.add(rel)
                w_loads[rel].wait()
                w_pair[rel].wait_recv()
            if k == 0:
                dy_pair[begin].wait_recv()
            part[way] = frozen(rel, begin, GROUP)
            if k >= 2:
                z_copies[way, m - 2 * pieces].wait_recv()

            def move(n, carry):
                rows = pl.ds(pl.multiple_of(j * GROUP + n * strip, strip), strip)
                v = part[way, pl.ds(pl.multiple_of(n * strip, strip), strip)]
                if k >= 2:
                    v = v + decode(z_in[way, k - 2, rows])
                z_out[way, k, rows] = encode(v)
                return carry

            lax.fori_loop(0, GROUP // strip, move, 0)
            z_copies[way, m].start()

    def z_steps(first, last):
        for m in range(first, last + 1):
            z_step(m)

    def z_end(way, k):
        begin = HALF[way][k] * half
        for j in range(pieces):
            z_copies[way, k * pieces + j].wait_recv()

        def move(n, carry):
            rows = pl.ds(pl.multiple_of(begin + n * strip, strip), strip)
            own[rows] = own[rows] + decode(z_in[way, k, pl.ds(pl.multiple_of(n * strip, strip), strip)])
            return carry

        lax.fori_loop(0, half // strip, move, 0)

    loads[2].wait()
    z_step(0)
    loads[0].wait()
    tables[0].start()
    loads[1].wait()
    tables[1].start()
    for table in tables:
        table.across(0)
    z_steps(1, 2)
    for table in tables:
        table.pass_first()
        table.across(3)
        table.across(1)

    def id_copy(k, place):
        return pltpu.make_async_remote_copy(
            src_ref=ids.at[dp],
            dst_ref=ids.at[place],
            send_sem=i_send.at[k],
            recv_sem=i_recv.at[k],
            device_id=(lax.rem(dp + k, OWNERS), tensor),
            device_id_type=MESH,
        )

    for k in range(1, OWNERS):
        id_copy(k, dp).start()
    z_steps(3, 5)
    for rel in (2, 6, 0):
        send_w(rel)
    for table in tables:
        table.end_first()
        table.across(2)
    for i in (0, 3, 1, 2):
        for table in tables:
            table.pass_second(i)
    z_step(6)
    for table in tables:
        table.end()
    for rel in (1, 7):
        send_w(rel)

    loads[3].wait()
    slots = [slot_of[adapter[g]] for g in range(groups)]
    downs, ups = [], []
    for s in slots:
        owner, at = lax.div(s, 4), lax.rem(s, 4)
        downs.append((place0(owner), at))
        ups.append((place1(owner), at))
    for g in range(groups):
        rows = pl.ds(g * GROUP, GROUP)
        dims = (((1,), (1,)), ((), ()))
        low = lax.dot_general(tab0[downs[g]], xv[rows], dims, preferred_element_type=F32)
        back = lax.dot_general(tab1[ups[g]], dyv[0, rows], dims, preferred_element_type=F32)
        rank_own[0, g] = low
        rank_own[1, g] = back
    rank_mate = to_mate(rank_own.at[1 - core], rank_pair, 8)
    rank_mate.start()
    z_step(7)
    rank_mate.wait_recv()
    rank_chip[...] = rank_own[core] + rank_pair[...]

    r_copies = []
    for k in range(1, DEPTH):
        copy = pltpu.make_async_remote_copy(
            src_ref=rank_chip.at[lax.rem(chip_z(k), groups)],
            dst_ref=rank_in.at[k],
            send_sem=r_send.at[k],
            recv_sem=r_recv.at[k],
            device_id=along_z(k),
            device_id_type=MESH,
        )
        copy.start()
        r_copies.append(copy)
    w_loads[0].wait()
    w_pair[0].wait_recv()
    for way in range(2):
        own[pl.ds(way * half, half)] = frozen(0, way * half, half)
    z_steps(8, 9)
    total = rank_chip[lax.rem(z, groups)]
    for k in range(1, DEPTH):
        r_copies[k - 1].wait_recv()
        total = total + rank_in[k]
    rank_all[core, z] = (total * jnp.where(core == 0, SCALE_DOWN, SCALE_UP).astype(F32)).astype(BF16)

    def a_copy(k, d):
        return pltpu.make_async_remote_copy(
            src_ref=rank_all.at[core, z],
            dst_ref=rank_all.at[core, chip_z(d)],
            send_sem=a_send.at[k],
            recv_sem=a_recv.at[k],
            device_id=along_z(k),
            device_id_type=MESH,
        )

    a_copies = [a_copy(k, 0) for k in range(1, DEPTH)]
    for copy in a_copies:
        copy.start()
    for k in range(1, OWNERS):
        id_copy(k, lax.rem(dp - k + OWNERS, OWNERS)).wait_recv()
    by_row = ids[...].reshape(OWNERS * 8, 128)
    by_column = by_row.T
    row = lax.broadcasted_iota(I32, by_row.shape, 0)
    column = lax.broadcasted_iota(I32, by_row.shape, 1)
    before = jnp.where((by_row == by_column) & (row < column), row, -1)
    last = jnp.where(by_row == column, row, -1)
    links_v[0:1] = jnp.max(before, axis=0, keepdims=True)
    links_v[1:2] = jnp.max(last, axis=0, keepdims=True)
    links = pltpu.make_async_copy(links_v, links_s, local_sem.at[12])
    links.start()

    z_steps(10, 13)
    for k in range(1, DEPTH):
        a_copy(k, -k).wait_recv()
    halves_out = to_mate(rank_all.at[core], rank_all.at[core], 9)
    halves_out.start()
    z_step(14)
    to_mate(rank_all.at[core], rank_all.at[1 - core], 9).wait_recv()

    def low_of(g):
        return rank_all[0, g]

    def back_of(g):
        return rank_all[1, g]

    row = lax.broadcasted_iota(I32, (8, 128), 0)
    most0, most1 = jnp.zeros((8, 128), F32), jnp.zeros((8, 128), F32)
    for g in range(groups):
        rows = pl.ds(g * GROUP, GROUP)
        code, high = encode_block(jnp.dot(back_of(g), xv[rows], preferred_element_type=F32) * SCALE_DOWN)
        code0[0, g] = code
        most0 = jnp.where(row == g, high, most0)
        code, high = encode_block(jnp.dot(low_of(g), dyv[0, rows], preferred_element_type=F32) * SCALE_UP)
        code1[0, g] = code
        most1 = jnp.where(row == g, high, most1)
    most[dp, 0:8] = most0
    most[dp, 8:16] = most1
    grads = (
        Gather(code0, g0_send, g0_recv, along_x, along_y, groups // 2),
        Gather(code1, g1_send, g1_recv, along_y, along_x, groups // 2),
    )
    for grad in grads:
        grad.start()
    for grad in grads:
        grad.across(0)

    def most_copy(k, place):
        return pltpu.make_async_remote_copy(
            src_ref=most.at[dp],
            dst_ref=most.at[place],
            send_sem=m_send.at[k],
            recv_sem=m_recv.at[k],
            device_id=(lax.rem(dp + k, OWNERS), tensor),
            device_id_type=MESH,
        )

    for k in range(1, OWNERS):
        most_copy(k, dp).start()
    for g in range(groups):
        rows = pl.ds(g * GROUP, GROUP)
        term = lax.dot_general(back_of(g), tab0[downs[g]], (((0,), (0,)), ((), ())), preferred_element_type=F32)
        own[rows] = own[rows] + term * SCALE_DOWN

    z_step(15)
    for grad in grads:
        grad.pass_first()
        grad.across(3)
        grad.across(1)
    z_step(16)
    for grad in grads:
        grad.pass_second(0)
    for grad in grads:
        grad.end_first()
        grad.across(2)
    z_step(17)
    for grad in grads:
        grad.pass_second(3)
    z_step(18)
    for grad in grads:
        grad.pass_second(1)
    z_step(19)
    for grad in grads:
        grad.pass_second(2)
    z_step(20)
    for grad in grads:
        grad.end()
    for k in range(1, OWNERS):
        most_copy(k, lax.rem(dp - k + OWNERS, OWNERS)).wait_recv()
    links.wait()

    def add_owner(d, carry):
        for g in range(groups):
            link = links_s[0, d * 8 + g]
            keep = jnp.where(link >= 0, 1.0, 0.0).astype(F32)
            link = jnp.maximum(link, 0)
            owner, at = lax.div(link, 8), lax.rem(link, 8)
            sum0[d, g] = decode_block(code0[place0(d), g], most[d, g : g + 1]) + keep * sum0[owner, at]
            sum1[d, g] = decode_block(code1[place1(d), g], most[d, 8 + g : 9 + g]) + keep * sum1[owner, at]
        return carry

    sum0[0, 0] = jnp.zeros(sum0.shape[2:], F32)
    sum1[0, 0] = jnp.zeros(sum1.shape[2:], F32)
    lax.fori_loop(0, OWNERS, add_owner, 0)

    def step_slot(s, carry):
        link = links_s[1, s]
        keep = jnp.where(link >= 0, LEARNING_RATE, 0.0).astype(F32)
        link = jnp.maximum(link, 0)
        owner, at = lax.div(link, 8), lax.rem(link, 8)
        home, spot = lax.div(s, 4), lax.rem(s, 4)
        out0[s] = (tab0[place0(home), spot].astype(F32) - keep * sum0[owner, at]).astype(BF16)
        out1[s] = (tab1[place1(home), spot].astype(F32) - keep * sum1[owner, at]).astype(BF16)
        return carry

    lax.fori_loop(0, out0.shape[0], step_slot, 0)
    stores = [
        pltpu.make_async_copy(out0, down_out, local_sem.at[13]),
        pltpu.make_async_copy(out1, up_out, local_sem.at[14]),
    ]
    for copy in stores:
        copy.start()
    for way in range(2):
        z_end(way, 5)
    stores.append(pltpu.make_async_copy(own, own_out, local_sem.at[15]))
    stores[-1].start()
    for way in range(2):
        for j in range(pieces):
            z_copies[way, (HOPS - 1) * pieces + j].wait_recv()
    for copy in [*dy_pair.values(), rank_mate, halves_out, *w_pair.values(), *z_copies.values(), *r_copies, *a_copies]:
        copy.wait_send()
    for k in range(1, OWNERS):
        id_copy(k, dp).wait_send()
        most_copy(k, dp).wait_send()
    for gather in [*tables, *grads]:
        gather.drain()
    for copy in stores:
        copy.wait()


PIECES = 6


def finish_kernel(own, last, down, up, token_out, down_out, up_out, total, sem):
    stores = [
        pltpu.make_async_copy(down, down_out, sem.at[PIECES]),
        pltpu.make_async_copy(up, up_out, sem.at[PIECES + 1]),
    ]
    for copy in stores:
        copy.start()
    size = total.shape[0] // PIECES
    for c in range(PIECES):
        rows = pl.ds(c * size, size)
        total[rows] = own[rows] + decode(last[rows])
        copy = pltpu.make_async_copy(total.at[rows], token_out.at[rows], sem.at[c])
        copy.start()
        stores.append(copy)
    for copy in stores:
        copy.wait()


def finish(own, last, down, up):
    any_space = pl.BlockSpec(memory_space=pl.ANY)
    return pl.pallas_call(
        finish_kernel,
        out_shape=tuple(jax.ShapeDtypeStruct(a.shape, a.dtype) for a in (own, down, up)),
        in_specs=[pl.BlockSpec(memory_space=pltpu.VMEM)] * 4,
        out_specs=(any_space,) * 3,
        scratch_shapes=[pltpu.VMEM(own.shape, F32), pltpu.SemaphoreType.DMA((PIECES + 2,))],
        compiler_params=pltpu.CompilerParams(vmem_limit_bytes=16 * 1024 * 1024),
        name="finish",
    )(own, last, down, up)


def shards(x, dy, w, down, up, adapter, slot_of):
    tokens, width = x.shape
    owned, rank, _ = down.shape
    groups = adapter.shape[0]
    slots = owned * OWNERS
    any_space = pl.BlockSpec(memory_space=pl.ANY)
    dma = pltpu.SemaphoreType.DMA
    vmem = pltpu.VMEM
    own, last, stepped_down, stepped_up = pl.pallas_call(
        kernel,
        out_shape=(
            vmem((tokens, width), F32),
            vmem((2, tokens // 2, width), BF16),
            vmem((slots, rank, width), BF16),
            vmem((slots, rank, width), BF16),
        ),
        in_specs=[pl.BlockSpec(memory_space=pltpu.HBM)] * 7,
        out_specs=(any_space,) * 4,
        scratch_shapes=[
            vmem((tokens, width), BF16),
            vmem((2, tokens, width), BF16),
            vmem((2, DEPTH, width, width), BF16),
            vmem((OWNERS, owned, rank, width), BF16),
            vmem((OWNERS, owned, rank, width), BF16),
            vmem((OWNERS, groups, rank, width), BF16),
            vmem((OWNERS, groups, rank, width), BF16),
            vmem((OWNERS, 16, 128), F32),
            vmem((OWNERS, groups, rank, width), F32),
            vmem((OWNERS, groups, rank, width), F32),
            vmem((OWNERS, 8, 128), I32),
            vmem((2, HOPS, tokens // 2, width), BF16),
            vmem((2, HOPS, tokens // 2, width), BF16),
            vmem((2, GROUP, width), F32),
            vmem((tokens, width), F32),
            vmem((2, groups, RANK, GROUP), F32),
            vmem((groups, RANK, GROUP), F32),
            vmem((groups, RANK, GROUP), F32),
            vmem((DEPTH, RANK, GROUP), F32),
            vmem((2, DEPTH, RANK, GROUP), BF16),
            vmem((slots, rank, width), BF16),
            vmem((slots, rank, width), BF16),
            vmem((8, 128), I32),
            pltpu.SMEM((8, 128), I32),
            pltpu.SMEM(adapter.shape, I32),
            pltpu.SMEM(slot_of.shape, I32),
            dma((18,)),
            dma((10 + groups,)),
            dma((10 + groups,)),
        ]
        + [dma((20,))] * 8
        + [dma((2, HOPS * (tokens // 2 // GROUP)))] * 2
        + [dma((DEPTH,))] * 4
        + [dma((OWNERS,))] * 4,
        compiler_params=pltpu.CompilerParams(
            collective_id=0, has_side_effects=True, vmem_limit_bytes=51 * 1024 * 1024
        ),
        name="lora_step",
    )(x, dy, w, down, up, adapter, slot_of)
    return finish(own, last.reshape(tokens, width), stepped_down, stepped_up)


def solution(mesh):
    return jax.shard_map(
        shards,
        mesh=mesh,
        in_specs=(
            P("dp", "tensor"),
            P("dp", "tensor"),
            P(None, "tensor"),
            P("dp", None, "tensor"),
            P("dp", None, "tensor"),
            P("dp"),
            P(),
        ),
        out_specs=(P("dp", "tensor"), P(None, None, "tensor"), P(None, None, "tensor")),
        check_vma=False,
    )
```

```python
import math

import jax
import jax.numpy as jnp
from jax import lax
from jax.experimental import pallas as pl
from jax.experimental.pallas import tpu as pltpu
from jax.sharding import PartitionSpec as P

MODEL_WIDTH = 8192
RANK = 16
GROUP = 128
ADAPTER_SCALE = 0.25
LEARNING_RATE = 1.5
SCALE_DOWN = 1.0 / math.sqrt(MODEL_WIDTH)
SCALE_UP = ADAPTER_SCALE / math.sqrt(RANK)

SIDE = 4
DEPTH = 8
OWNERS = SIDE * SIDE

POWER_SHIFT = 19.0

MESH = pl.DeviceIdType.MESH
F32 = jnp.float32
BF16 = jnp.bfloat16
I32 = jnp.int32
HOPS = 7
TARGET = ((4, 3, 3, 2, 2, 1, 1), (4, 5, 5, 6, 6, 7, 7))
HALF = ((0, 1, 0, 1, 0, 1, 0), (1, 0, 1, 0, 1, 0, 1))
W_ORDER = (4, 3, 5, 2, 6, 1, 7, 0)


def encode(v):
    u = v * (2.0**POWER_SHIFT)
    return ((u * jnp.abs(u)) * (u * u)).astype(BF16)


def decode(code):
    w = code.astype(F32)
    root = jnp.exp2(jnp.log(jnp.abs(w)) * (0.25 / math.log(2.0)) - POWER_SHIFT)
    return jnp.where(w < 0, -root, root)


BLOCK_SHIFT = 7.8


def encode_block(v):
    most = jnp.maximum(jnp.max(jnp.max(jnp.abs(v), axis=0, keepdims=True), axis=1, keepdims=True), 1e-30)
    u = v * (2.0**BLOCK_SHIFT / most)
    u2 = u * u
    u4 = u2 * u2
    return (((u4 * u4) * u4) * (u2 * (u * jnp.abs(u)))).astype(BF16), most


def decode_block(code, most):
    w = code.astype(F32)
    root = jnp.exp2(jnp.log(jnp.abs(w)) * (0.0625 / math.log(2.0)) - BLOCK_SHIFT)
    return jnp.where(w < 0, -root, root) * jnp.concatenate([most] * (w.shape[1] // 128), axis=1)


class Gather:
    def __init__(self, buf, send, recv, first, second, cut):
        self.buf, self.send, self.recv, self.first, self.second = buf, send, recv, first, second
        rows = buf.shape[1]
        self.parts = {"all": (0, rows), "a": (0, cut), "b": (cut, rows - cut)}
        self.copies = {}

    def go(self, number, device, source, target, part):
        begin, size = self.parts[part]
        copy = pltpu.make_async_remote_copy(
            src_ref=self.buf.at[source, pl.ds(begin, size)],
            dst_ref=self.buf.at[target, pl.ds(begin, size)],
            send_sem=self.send.at[number],
            recv_sem=self.recv.at[number],
            device_id=device,
            device_id_type=MESH,
        )
        copy.start()
        self.copies[number] = copy

    def wait(self, number):
        self.copies[number].wait_recv()

    def start(self):
        self.go(0, self.first(1), 0, 12, "all")
        self.go(1, self.first(-1), 0, 4, "all")

    def across(self, i):
        self.go(4 + 4 * i, self.second(1), 4 * i, 4 * i + 3, "all")
        self.go(5 + 4 * i, self.second(-1), 4 * i, 4 * i + 1, "all")

    def pass_first(self):
        self.wait(0)
        self.go(2, self.first(1), 12, 8, "a")
        self.wait(1)
        self.go(3, self.first(-1), 4, 8, "b")

    def end_first(self):
        self.wait(2)
        self.wait(3)

    def pass_second(self, i):
        self.wait(4 + 4 * i)
        self.go(6 + 4 * i, self.second(1), 4 * i + 3, 4 * i + 2, "a")
        self.wait(5 + 4 * i)
        self.go(7 + 4 * i, self.second(-1), 4 * i + 1, 4 * i + 2, "b")

    def end(self):
        for i in range(SIDE):
            self.wait(6 + 4 * i)
            self.wait(7 + 4 * i)

    def drain(self):
        for copy in self.copies.values():
            copy.wait_send()


def kernel(
    x_hbm,
    dy_hbm,
    w_hbm,
    down_hbm,
    up_hbm,
    adapter_hbm,
    slot_of_hbm,
    own_out,
    last_out,
    down_out,
    up_out,
    xv,
    dyv,
    wv,
    tab0,
    tab1,
    code0,
    code1,
    most,
    sum0,
    sum1,
    ids,
    z_in,
    z_out,
    part,
    own,
    rank_own,
    rank_pair,
    rank_chip,
    rank_in,
    rank_all,
    out0,
    out1,
    links_v,
    links_s,
    adapter,
    slot_of,
    local_sem,
    pair_send,
    pair_recv,
    t0_send,
    t0_recv,
    t1_send,
    t1_recv,
    g0_send,
    g0_recv,
    g1_send,
    g1_recv,
    z_send,
    z_recv,
    r_send,
    r_recv,
    a_send,
    a_recv,
    i_send,
    i_recv,
    m_send,
    m_recv,
):
    dp, tensor = lax.axis_index("dp"), lax.axis_index("tensor")
    x, y = lax.div(dp, SIDE), lax.rem(dp, SIDE)
    z, core = lax.div(tensor, 2), lax.rem(tensor, 2)
    tokens, width = own.shape
    half = tokens // 2
    groups = tokens // GROUP
    mate = (dp, z * 2 + 1 - core)

    def along_x(d):
        return (lax.rem(x + d + SIDE, SIDE) * SIDE + y, tensor)

    def along_y(d):
        return (x * SIDE + lax.rem(y + d + SIDE, SIDE), tensor)

    def chip_z(d):
        return lax.rem(z + d + DEPTH, DEPTH)

    def along_z(d):
        return (dp, chip_z(d) * 2 + core)

    def place0(owner):
        i = lax.rem(lax.div(owner, SIDE) - x + SIDE, SIDE)
        return i * SIDE + lax.rem(lax.rem(owner, SIDE) - y + SIDE, SIDE)

    def place1(owner):
        i = lax.rem(lax.rem(owner, SIDE) - y + SIDE, SIDE)
        return i * SIDE + lax.rem(lax.div(owner, SIDE) - x + SIDE, SIDE)

    def w_rows(rel, parity):
        begin = pl.multiple_of((chip_z(rel) * 2 + parity) * width, width)
        return w_hbm.at[pl.ds(begin, width)]

    loads = [
        pltpu.make_async_copy(down_hbm, tab0.at[0], local_sem.at[0]),
        pltpu.make_async_copy(up_hbm, tab1.at[0], local_sem.at[1]),
        pltpu.make_async_copy(dy_hbm, dyv.at[0], local_sem.at[2]),
        pltpu.make_async_copy(x_hbm, xv, local_sem.at[3]),
    ]
    w_loads = {rel: pltpu.make_async_copy(w_rows(rel, core), wv.at[0, rel], local_sem.at[4 + rel]) for rel in W_ORDER}
    ids_loads = [
        pltpu.make_async_copy(adapter_hbm, adapter, local_sem.at[16]),
        pltpu.make_async_copy(slot_of_hbm, slot_of, local_sem.at[17]),
    ]
    for copy in ids_loads:
        copy.start()
    w_loads[4].start()
    loads[2].start()
    loads[0].start()
    loads[1].start()
    loads[3].start()
    for rel in W_ORDER[1:]:
        w_loads[rel].start()

    for copy in ids_loads:
        copy.wait()
    row = lax.broadcasted_iota(I32, (8, 128), 0)
    tile = jnp.full((8, 128), -1, I32)
    for g in range(groups):
        tile = jnp.where(row == g, slot_of[adapter[g]], tile)
    ids[dp] = tile

    barrier = pltpu.get_barrier_semaphore()
    pl.semaphore_signal(barrier, inc=1, device_id=mate, device_id_type=MESH)
    for k in range(1, DEPTH):
        pl.semaphore_signal(barrier, inc=1, device_id=along_z(k), device_id_type=MESH)
    for k in range(1, OWNERS):
        pl.semaphore_signal(barrier, inc=1, device_id=(lax.rem(dp + k, OWNERS), tensor), device_id_type=MESH)
    pl.semaphore_wait(barrier, DEPTH + OWNERS - 1)

    def to_mate(source, target, number):
        return pltpu.make_async_remote_copy(
            src_ref=source,
            dst_ref=target,
            send_sem=pair_send.at[number],
            recv_sem=pair_recv.at[number],
            device_id=mate,
            device_id_type=MESH,
        )

    w_pair = {rel: to_mate(w_rows(rel, 1 - core), wv.at[1, rel], rel) for rel in W_ORDER}

    def send_w(rel):
        begin = (chip_z(rel) * 2 + 1 - core) * width
        for n in range(0, width, GROUP):
            source = w_hbm.at[pl.ds(pl.multiple_of(begin + n, GROUP), GROUP)]
            to_mate(source, wv.at[1, rel, pl.ds(n, GROUP)], rel).start()

    send_w(4)
    dy_pair = {}
    for c in range(half // GROUP):
        for begin in (c * GROUP, half + c * GROUP):
            rows = pl.ds(begin, GROUP)
            dy_pair[begin] = to_mate(dy_hbm.at[rows], dyv.at[1, rows], 10 + begin // GROUP)
            dy_pair[begin].start()

    tables = (
        Gather(tab0, t0_send, t0_recv, along_x, along_y, 2),
        Gather(tab1, t1_send, t1_recv, along_y, along_x, 2),
    )
    send_w(3)
    send_w(5)

    def frozen(rel, begin, size):
        rows = pl.ds(begin, size)
        dims = (((1,), (1,)), ((), ()))
        first = lax.dot_general(dyv[0, rows], wv[0, rel], dims, preferred_element_type=F32)
        second = lax.dot_general(dyv[1, rows], wv[1, rel], dims, preferred_element_type=F32)
        return first + second

    pieces = half // GROUP

    def z_copy(way, m):
        k, rows = m // pieces, pl.ds(m % pieces * GROUP, GROUP)
        return pltpu.make_async_remote_copy(
            src_ref=z_out.at[way, k, rows],
            dst_ref=z_in.at[way, k, rows] if k < HOPS - 1 else last_out.at[way, rows],
            send_sem=z_send.at[way, m],
            recv_sem=z_recv.at[way, m],
            device_id=along_z(1 - 2 * way),
            device_id_type=MESH,
        )

    z_copies = {(way, m): z_copy(way, m) for way in range(2) for m in range(HOPS * pieces)}
    strip = 64
    have = set()

    def z_step(m):
        k, j = m // pieces, m % pieces
        for way in range(2):
            rel, begin = TARGET[way][k], HALF[way][k] * half + j * GROUP
            if rel not in have:
                have.add(rel)
                w_loads[rel].wait()
                w_pair[rel].wait_recv()
            if k == 0:
                dy_pair[begin].wait_recv()
            part[way] = frozen(rel, begin, GROUP)
            if k >= 2:
                z_copies[way, m - 2 * pieces].wait_recv()

            def move(n, carry):
                rows = pl.ds(pl.multiple_of(j * GROUP + n * strip, strip), strip)
                v = part[way, pl.ds(pl.multiple_of(n * strip, strip), strip)]
                if k >= 2:
                    v = v + decode(z_in[way, k - 2, rows])
                z_out[way, k, rows] = encode(v)
                return carry

            lax.fori_loop(0, GROUP // strip, move, 0)
            z_copies[way, m].start()

    def z_steps(first, last):
        for m in range(first, last + 1):
            z_step(m)

    def z_end(way, k):
        begin = HALF[way][k] * half
        for j in range(pieces):
            z_copies[way, k * pieces + j].wait_recv()

        def move(n, carry):
            rows = pl.ds(pl.multiple_of(begin + n * strip, strip), strip)
            own[rows] = own[rows] + decode(z_in[way, k, pl.ds(pl.multiple_of(n * strip, strip), strip)])
            return carry

        lax.fori_loop(0, half // strip, move, 0)

    loads[2].wait()
    z_step(0)
    loads[0].wait()
    tables[0].start()
    loads[1].wait()
    tables[1].start()
    for table in tables:
        table.across(0)
    z_steps(1, 2)
    for table in tables:
        table.pass_first()
        table.across(3)
        table.across(1)

    def id_copy(k, place):
        return pltpu.make_async_remote_copy(
            src_ref=ids.at[dp],
            dst_ref=ids.at[place],
            send_sem=i_send.at[k],
            recv_sem=i_recv.at[k],
            device_id=(lax.rem(dp + k, OWNERS), tensor),
            device_id_type=MESH,
        )

    for k in range(1, OWNERS):
        id_copy(k, dp).start()
    z_steps(3, 5)
    for rel in (2, 6, 0):
        send_w(rel)
    for table in tables:
        table.end_first()
        table.across(2)
    for i in (0, 3, 1, 2):
        for table in tables:
            table.pass_second(i)
    z_step(6)
    for table in tables:
        table.end()
    for rel in (1, 7):
        send_w(rel)

    loads[3].wait()
    slots = [slot_of[adapter[g]] for g in range(groups)]
    downs, ups = [], []
    for s in slots:
        owner, at = lax.div(s, 4), lax.rem(s, 4)
        downs.append((place0(owner), at))
        ups.append((place1(owner), at))
    for g in range(groups):
        rows = pl.ds(g * GROUP, GROUP)
        dims = (((1,), (1,)), ((), ()))
        low = lax.dot_general(tab0[downs[g]], xv[rows], dims, preferred_element_type=F32)
        back = lax.dot_general(tab1[ups[g]], dyv[0, rows], dims, preferred_element_type=F32)
        rank_own[0, g] = low
        rank_own[1, g] = back
    rank_mate = to_mate(rank_own.at[1 - core], rank_pair, 8)
    rank_mate.start()
    z_step(7)
    rank_mate.wait_recv()
    rank_chip[...] = rank_own[core] + rank_pair[...]

    far_first = (4, 3, 5, 2, 6, 1, 7)

    def r_copy(k):
        return pltpu.make_async_remote_copy(
            src_ref=rank_chip.at[lax.rem(chip_z(k), groups)],
            dst_ref=rank_in.at[k],
            send_sem=r_send.at[k],
            recv_sem=r_recv.at[k],
            device_id=along_z(k),
            device_id_type=MESH,
        )

    for k in far_first:

        @pl.when(chip_z(k) < groups)
        def _():
            r_copy(k).start()

    w_loads[0].wait()
    w_pair[0].wait_recv()
    for way in range(2):
        own[pl.ds(way * half, half)] = frozen(0, way * half, half)
    z_steps(8, 9)
    @pl.when(z < groups)
    def _():
        total = rank_chip[z]
        for k in range(1, DEPTH):
            r_copy(k).wait_recv()
            total = total + rank_in[k]
        rank_all[core, z] = (total * jnp.where(core == 0, SCALE_DOWN, SCALE_UP).astype(F32)).astype(BF16)

    def a_copy(k, d):
        return pltpu.make_async_remote_copy(
            src_ref=rank_all.at[core, z],
            dst_ref=rank_all.at[core, chip_z(d)],
            send_sem=a_send.at[k],
            recv_sem=a_recv.at[k],
            device_id=along_z(k),
            device_id_type=MESH,
        )

    @pl.when(z < groups)
    def _():
        for k in far_first:
            a_copy(k, 0).start()

    for k in range(1, OWNERS):
        id_copy(k, lax.rem(dp - k + OWNERS, OWNERS)).wait_recv()
    by_row = ids[...].reshape(OWNERS * 8, 128)
    by_column = by_row.T
    row = lax.broadcasted_iota(I32, by_row.shape, 0)
    column = lax.broadcasted_iota(I32, by_row.shape, 1)
    before = jnp.where((by_row == by_column) & (row < column), row, -1)
    last = jnp.where(by_row == column, row, -1)
    links_v[0:1] = jnp.max(before, axis=0, keepdims=True)
    links_v[1:2] = jnp.max(last, axis=0, keepdims=True)
    links = pltpu.make_async_copy(links_v, links_s, local_sem.at[12])
    links.start()

    z_steps(10, 13)
    for k in range(1, DEPTH):

        @pl.when(chip_z(-k) < groups)
        def _():
            a_copy(k, -k).wait_recv()

    sums = pl.ds(0, groups)
    halves_out = to_mate(rank_all.at[core, sums], rank_all.at[core, sums], 9)
    halves_out.start()
    z_step(14)
    to_mate(rank_all.at[core, sums], rank_all.at[1 - core, sums], 9).wait_recv()

    def low_of(g):
        return rank_all[0, g]

    def back_of(g):
        return rank_all[1, g]

    row = lax.broadcasted_iota(I32, (8, 128), 0)
    most0, most1 = jnp.zeros((8, 128), F32), jnp.zeros((8, 128), F32)
    for g in range(groups):
        rows = pl.ds(g * GROUP, GROUP)
        code, high = encode_block(jnp.dot(back_of(g), xv[rows], preferred_element_type=F32) * SCALE_DOWN)
        code0[0, g] = code
        most0 = jnp.where(row == g, high, most0)
        code, high = encode_block(jnp.dot(low_of(g), dyv[0, rows], preferred_element_type=F32) * SCALE_UP)
        code1[0, g] = code
        most1 = jnp.where(row == g, high, most1)
    most[dp, 0:8] = most0
    most[dp, 8:16] = most1
    grads = (
        Gather(code0, g0_send, g0_recv, along_x, along_y, groups // 2),
        Gather(code1, g1_send, g1_recv, along_y, along_x, groups // 2),
    )
    for grad in grads:
        grad.start()
    for grad in grads:
        grad.across(0)

    def most_copy(k, place):
        return pltpu.make_async_remote_copy(
            src_ref=most.at[dp],
            dst_ref=most.at[place],
            send_sem=m_send.at[k],
            recv_sem=m_recv.at[k],
            device_id=(lax.rem(dp + k, OWNERS), tensor),
            device_id_type=MESH,
        )

    for k in range(1, OWNERS):
        most_copy(k, dp).start()
    for g in range(groups):
        rows = pl.ds(g * GROUP, GROUP)
        term = lax.dot_general(back_of(g), tab0[downs[g]], (((0,), (0,)), ((), ())), preferred_element_type=F32)
        own[rows] = own[rows] + term * SCALE_DOWN

    z_step(15)
    for grad in grads:
        grad.pass_first()
        grad.across(3)
        grad.across(1)
    z_step(16)
    for grad in grads:
        grad.pass_second(0)
    for grad in grads:
        grad.end_first()
        grad.across(2)
    z_step(17)
    for grad in grads:
        grad.pass_second(3)
    z_step(18)
    for grad in grads:
        grad.pass_second(1)
    z_step(19)
    for grad in grads:
        grad.pass_second(2)
    z_step(20)
    for grad in grads:
        grad.end()
    for k in range(1, OWNERS):
        most_copy(k, lax.rem(dp - k + OWNERS, OWNERS)).wait_recv()
    links.wait()

    def add_owner(d, carry):
        for g in range(groups):
            link = links_s[0, d * 8 + g]
            keep = jnp.where(link >= 0, 1.0, 0.0).astype(F32)
            link = jnp.maximum(link, 0)
            owner, at = lax.div(link, 8), lax.rem(link, 8)
            sum0[d, g] = decode_block(code0[place0(d), g], most[d, g : g + 1]) + keep * sum0[owner, at]
            sum1[d, g] = decode_block(code1[place1(d), g], most[d, 8 + g : 9 + g]) + keep * sum1[owner, at]
        return carry

    sum0[0, 0] = jnp.zeros(sum0.shape[2:], F32)
    sum1[0, 0] = jnp.zeros(sum1.shape[2:], F32)
    lax.fori_loop(0, OWNERS, add_owner, 0)

    def step_slot(s, carry):
        link = links_s[1, s]
        keep = jnp.where(link >= 0, LEARNING_RATE, 0.0).astype(F32)
        link = jnp.maximum(link, 0)
        owner, at = lax.div(link, 8), lax.rem(link, 8)
        home, spot = lax.div(s, 4), lax.rem(s, 4)
        out0[s] = (tab0[place0(home), spot].astype(F32) - keep * sum0[owner, at]).astype(BF16)
        out1[s] = (tab1[place1(home), spot].astype(F32) - keep * sum1[owner, at]).astype(BF16)
        return carry

    lax.fori_loop(0, out0.shape[0], step_slot, 0)
    stores = [
        pltpu.make_async_copy(out0, down_out, local_sem.at[13]),
        pltpu.make_async_copy(out1, up_out, local_sem.at[14]),
    ]
    for copy in stores:
        copy.start()
    for way in range(2):
        z_end(way, 5)
    stores.append(pltpu.make_async_copy(own, own_out, local_sem.at[15]))
    stores[-1].start()
    for way in range(2):
        for j in range(pieces):
            z_copies[way, (HOPS - 1) * pieces + j].wait_recv()
    for copy in [*dy_pair.values(), rank_mate, halves_out, *w_pair.values(), *z_copies.values()]:
        copy.wait_send()
    for k in range(1, DEPTH):

        @pl.when(chip_z(k) < groups)
        def _():
            r_copy(k).wait_send()

        @pl.when(z < groups)
        def _():
            a_copy(k, 0).wait_send()

    for k in range(1, OWNERS):
        id_copy(k, dp).wait_send()
        most_copy(k, dp).wait_send()
    for gather in [*tables, *grads]:
        gather.drain()
    for copy in stores:
        copy.wait()


PIECES = 6


def finish_kernel(own, last, down, up, token_out, down_out, up_out, total, sem):
    stores = [
        pltpu.make_async_copy(down, down_out, sem.at[PIECES]),
        pltpu.make_async_copy(up, up_out, sem.at[PIECES + 1]),
    ]
    for copy in stores:
        copy.start()
    size = total.shape[0] // PIECES
    for c in range(PIECES):
        rows = pl.ds(c * size, size)
        total[rows] = own[rows] + decode(last[rows])
        copy = pltpu.make_async_copy(total.at[rows], token_out.at[rows], sem.at[c])
        copy.start()
        stores.append(copy)
    for copy in stores:
        copy.wait()


def finish(own, last, down, up):
    any_space = pl.BlockSpec(memory_space=pl.ANY)
    return pl.pallas_call(
        finish_kernel,
        out_shape=tuple(jax.ShapeDtypeStruct(a.shape, a.dtype) for a in (own, down, up)),
        in_specs=[pl.BlockSpec(memory_space=pltpu.VMEM)] * 4,
        out_specs=(any_space,) * 3,
        scratch_shapes=[pltpu.VMEM(own.shape, F32), pltpu.SemaphoreType.DMA((PIECES + 2,))],
        compiler_params=pltpu.CompilerParams(vmem_limit_bytes=16 * 1024 * 1024),
        name="finish",
    )(own, last, down, up)


def shards(x, dy, w, down, up, adapter, slot_of):
    tokens, width = x.shape
    owned, rank, _ = down.shape
    groups = adapter.shape[0]
    slots = owned * OWNERS
    any_space = pl.BlockSpec(memory_space=pl.ANY)
    dma = pltpu.SemaphoreType.DMA
    vmem = pltpu.VMEM
    own, last, stepped_down, stepped_up = pl.pallas_call(
        kernel,
        out_shape=(
            vmem((tokens, width), F32),
            vmem((2, tokens // 2, width), BF16),
            vmem((slots, rank, width), BF16),
            vmem((slots, rank, width), BF16),
        ),
        in_specs=[pl.BlockSpec(memory_space=pltpu.HBM)] * 7,
        out_specs=(any_space,) * 4,
        scratch_shapes=[
            vmem((tokens, width), BF16),
            vmem((2, tokens, width), BF16),
            vmem((2, DEPTH, width, width), BF16),
            vmem((OWNERS, owned, rank, width), BF16),
            vmem((OWNERS, owned, rank, width), BF16),
            vmem((OWNERS, groups, rank, width), BF16),
            vmem((OWNERS, groups, rank, width), BF16),
            vmem((OWNERS, 16, 128), F32),
            vmem((OWNERS, groups, rank, width), F32),
            vmem((OWNERS, groups, rank, width), F32),
            vmem((OWNERS, 8, 128), I32),
            vmem((2, HOPS, tokens // 2, width), BF16),
            vmem((2, HOPS, tokens // 2, width), BF16),
            vmem((2, GROUP, width), F32),
            vmem((tokens, width), F32),
            vmem((2, groups, RANK, GROUP), F32),
            vmem((groups, RANK, GROUP), F32),
            vmem((groups, RANK, GROUP), F32),
            vmem((DEPTH, RANK, GROUP), F32),
            vmem((2, DEPTH, RANK, GROUP), BF16),
            vmem((slots, rank, width), BF16),
            vmem((slots, rank, width), BF16),
            vmem((8, 128), I32),
            pltpu.SMEM((8, 128), I32),
            pltpu.SMEM(adapter.shape, I32),
            pltpu.SMEM(slot_of.shape, I32),
            dma((18,)),
            dma((10 + groups,)),
            dma((10 + groups,)),
        ]
        + [dma((20,))] * 8
        + [dma((2, HOPS * (tokens // 2 // GROUP)))] * 2
        + [dma((DEPTH,))] * 4
        + [dma((OWNERS,))] * 4,
        compiler_params=pltpu.CompilerParams(
            collective_id=0, has_side_effects=True, vmem_limit_bytes=51 * 1024 * 1024
        ),
        name="lora_step",
    )(x, dy, w, down, up, adapter, slot_of)
    return finish(own, last.reshape(tokens, width), stepped_down, stepped_up)


def solution(mesh):
    return jax.shard_map(
        shards,
        mesh=mesh,
        in_specs=(
            P("dp", "tensor"),
            P("dp", "tensor"),
            P(None, "tensor"),
            P("dp", None, "tensor"),
            P("dp", None, "tensor"),
            P("dp"),
            P(),
        ),
        out_specs=(P("dp", "tensor"), P(None, None, "tensor"), P(None, None, "tensor")),
        check_vma=False,
    )
```
